512 devices in a mesh: dp: 16 (over x_hi, z), tensor: 32 (over x_lo, y, core).
Axes of the slice: x: 4 (x_hi: 2, x_lo: 2; x = x_hi * 2 + x_lo), y: 8, z: 8, core: 2. Of those that a mesh axis runs over, the one named last changes fastest.
Arguments:
- tokens: bfloat16 [8192, 8192], P('dp', 'tensor'), may hold values from -6 to 6
- query_weight: bfloat16 [8192, 8192], P(None, 'tensor'), may hold values from -0.0625 to 0.0625
- adapter_down_weight: bfloat16 [64, 64, 8192], P('dp', None, 'tensor'), may hold values from -0.0625 to 0.0625
- adapter_up_weight: bfloat16 [64, 64, 8192], P('dp', None, 'tensor'), may hold values from -0.75 to 0.75
- segment_request: int32 [64], P('dp'), may hold values from 0 to 31, as said below
- request_adapter_ids: int32 [32], P('dp'), may hold values from 0 to 63
- adapter_stored_row: int32 [64], replicated, may hold values from 0 to 63, each once
Outputs:
- query: bfloat16 [8192, 8192], P('dp', 'tensor')
The draws below stay inside these ranges and needn't reach their ends.
Inputs may be any that keep to these rules, and one draw needn't show every extreme that they name: `segment_request`: segments of one request are consecutive; every request has one or more segments; the segments of dp index g name requests g * 2 to (g + 1) * 2 - 1.
All inputs are finite; a program needn't handle non-finite values.
Results may differ from the reference program's by a relative error of at most 0.0046.
Values may be sent and summed in bfloat16 or wider, within the bound.
No kernel may reach another device: no remote copies, remote signals or barrier semaphores. Data moves between devices by JAX's collectives and lax.ppermute only.
A program may use at most 64 MiB of HBM per device.

```python
import math
import jax
import jax.numpy as jnp
import numpy as np
from jax import lax

MODEL_WIDTH = 8192
QUERY_COLUMNS = 8192
ADAPTER_RANK = 64
SEG = 128
SEGS_DEV = 4
REQ_DEV = 2
TOKENS = 8192
SEGMENTS = 64
REQUESTS = 32
ADAPTER_COUNT = 64


def draw_segment_request(key, part):
    key = jax.random.fold_in(key, 11)
    groups = SEGMENTS // SEGS_DEV
    keys = jax.random.split(key, groups)

    def one_group(group_key):
        order = jax.random.permutation(group_key, SEGS_DEV - 1) + 1
        cuts = order[:REQ_DEV - 1]
        places = jnp.arange(SEGS_DEV)
        return jnp.sum((cuts[None, :] <= places[:, None]).astype(jnp.int32), axis=1)
    local = jax.vmap(one_group)(keys)
    offsets = jnp.arange(groups, dtype=jnp.int32)[:, None] * REQ_DEV
    return (local + offsets).reshape(-1).astype(jnp.int32)


def set_ends(result, key, least, high):
    spot = [jax.random.randint(jax.random.fold_in(key, axis), (), 0, length) for axis, length in enumerate(result.shape)]
    widest = result.shape.index(max(result.shape))
    beside = spot[:widest] + [(spot[widest] + 1) % result.shape[widest]] + spot[widest + 1:]
    return result.at[tuple(spot)].set(least).at[tuple(beside)].set(high)


def steps_of(stream_key, shape, cuts, low, largest):
    def one(position, parts):
        steps = jax.random.uniform(jax.random.fold_in(jax.random.fold_in(stream_key, 6), position), (parts,), jnp.float32, low / len(cuts), largest / len(cuts))
        return jnp.repeat(jnp.exp(steps), shape[position] // parts).reshape((-1,) + (1,) * (len(shape) - position - 1))

    level = one(*cuts[0])
    for cut in cuts[1:]:
        level = level * one(*cut)
    return level


def rank_bounds(number_of, slope):
    weights = [(1 << 20) // math.isqrt(standing ** slope) + 1 for standing in range(1, number_of + 1)]
    scale = 1 + sum(weights) // (1 << 30)
    return np.cumsum(np.array([max(1, weight // scale) for weight in weights]))


def skewed_ids(own_key, dims, count, slope):
    grid = rank_bounds(count, slope)
    pick = jax.random.randint(jax.random.fold_in(own_key, 1), dims, 0, int(grid[count - 1]))
    standing = jnp.searchsorted(jnp.asarray(grid, jnp.int32), pick, side="right")
    return jax.random.permutation(jax.random.fold_in(own_key, 2), count)[standing].astype(jnp.int32)


def centred(rng, extent, scale, reach, cuts=(), kind=jnp.bfloat16):
    level = steps_of(rng, extent, cuts, -0.22, 0.18) if cuts else 1.0
    values = jax.random.normal(rng, extent, jnp.float32) * scale * level
    return jnp.minimum(jnp.maximum(values, -reach), reach).astype(kind)


def setup_inputs(seed: int = 0) -> dict:
    seeds = jax.random.split(jax.random.key(seed), 8)
    tokens = centred(seeds[0], (TOKENS, MODEL_WIDTH), 1.0, 6.0, ((0, 16), (1, 32)))
    query_weight = centred(seeds[1], (MODEL_WIDTH, QUERY_COLUMNS), MODEL_WIDTH ** -0.5, 0.0625, ((1, 32),))
    adapter_down_weight = centred(seeds[2], (ADAPTER_COUNT, ADAPTER_RANK, MODEL_WIDTH), MODEL_WIDTH ** -0.5, 0.0625, ((0, 16), (2, 32)))
    adapter_up_weight = centred(seeds[3], (ADAPTER_COUNT, ADAPTER_RANK, QUERY_COLUMNS), ADAPTER_RANK ** -0.5, 0.75, ((0, 16), (2, 32)))
    segment_request = draw_segment_request(jax.random.fold_in(seeds[7], 71), 0)
    request_adapter_ids = set_ends(skewed_ids(seeds[5], (REQUESTS,), ADAPTER_COUNT, 2), jax.random.fold_in(seeds[5], 3), 0, ADAPTER_COUNT - 1).astype(jnp.int32)
    adapter_stored_row = jax.random.permutation(seeds[6], ADAPTER_COUNT).astype(jnp.int32)
    return {"tokens": tokens, "query_weight": query_weight, "adapter_down_weight": adapter_down_weight, "adapter_up_weight": adapter_up_weight, "segment_request": segment_request, "request_adapter_ids": request_adapter_ids, "adapter_stored_row": adapter_stored_row}


adapter_scale = 2.0


def reference(tokens, query_weight, adapter_down_weight, adapter_up_weight, segment_request, request_adapter_ids, adapter_stored_row):
    base_output = jnp.dot(tokens, query_weight, preferred_element_type=jnp.float32)
    storage_rows = adapter_stored_row[request_adapter_ids[segment_request]].astype(jnp.int32)
    segment_rows = tokens.reshape(SEGMENTS, SEG, MODEL_WIDTH)

    def one_segment(items):
        block, segment_index = items
        down_product = lax.dynamic_index_in_dim(adapter_down_weight, segment_index, 0, keepdims=False)
        up_product = lax.dynamic_index_in_dim(adapter_up_weight, segment_index, 0, keepdims=False)
        lowrank = lax.dot_general(block, down_product, (((1,), (1,)), ((), ())), preferred_element_type=jnp.float32)
        lowrank = lowrank.astype(jnp.bfloat16)
        return jnp.dot(lowrank, up_product, preferred_element_type=jnp.float32)

    adapter_output = lax.map(one_segment, (segment_rows, storage_rows)).reshape(TOKENS, QUERY_COLUMNS)
    return (base_output + adapter_scale * adapter_output).astype(jnp.bfloat16)
```

```python
import jax
import jax.numpy as jnp
from jax import lax
from jax.experimental import pallas as pl
from jax.experimental.pallas import tpu as pltpu
from jax.sharding import Mesh, PartitionSpec as P

SWAP = [(0, 1), (1, 0)]
DP = ("xh", "z")
TENSOR = ("xl", "y", "c")
ROWS = 512
SEG = 128
RANK = 64
WIDTH = 256
OWNED = 4


def select_kernel(rows_ref, me_ref, mats_ref, out_ref):
    first = me_ref[0] * OWNED

    def step(i, carry):
        slot = jnp.clip(rows_ref[i] - first, 0, OWNED - 1)
        out_ref[i] = mats_ref[slot]
        return carry

    lax.fori_loop(0, out_ref.shape[0], step, 0)


def select(rows, me, mats):
    count = rows.shape[0]
    return pl.pallas_call(
        select_kernel,
        out_shape=jax.ShapeDtypeStruct((count,) + mats.shape[1:], mats.dtype),
        in_specs=[
            pl.BlockSpec(memory_space=pltpu.SMEM),
            pl.BlockSpec(memory_space=pltpu.SMEM),
            pl.BlockSpec(memory_space=pltpu.VMEM),
        ],
        out_specs=pl.BlockSpec(memory_space=pltpu.VMEM),
        cost_estimate=pl.CostEstimate(flops=0, bytes_accessed=2 << 20, transcendentals=0),
    )(rows, me, mats)


def down_kernel(pick_ref, tokens_ref, mats_ref, out_ref):
    for k in range(4):
        mat = mats_ref[pick_ref[k]]
        part = lax.dot_general(
            tokens_ref[k * SEG : (k + 1) * SEG, :],
            mat,
            (((1,), (1,)), ((), ())),
            preferred_element_type=jnp.float32,
        )
        row, col = (k % 2) * SEG, (k // 2) * RANK
        out_ref[row : row + SEG, col : col + RANK] = part


def down_product(pick, tokens, mats):
    return pl.pallas_call(
        down_kernel,
        out_shape=jax.ShapeDtypeStruct((256, 128), jnp.float32),
        in_specs=[
            pl.BlockSpec(memory_space=pltpu.SMEM),
            pl.BlockSpec(memory_space=pltpu.VMEM),
            pl.BlockSpec(memory_space=pltpu.VMEM),
        ],
        out_specs=pl.BlockSpec(memory_space=pltpu.VMEM),
        cost_estimate=pl.CostEstimate(flops=1 << 24, bytes_accessed=1 << 20, transcendentals=0),
    )(pick, tokens, mats)


def main_kernel(pick_ref, low_ref, mats_ref, t_ref, w_ref, out_ref, acc_ref):
    step = pl.program_id(0)
    part = jnp.dot(t_ref[...], w_ref[...], preferred_element_type=jnp.float32)

    @pl.when(step == 0)
    def _():
        for k in range(4):
            row, col = (k % 2) * SEG, (k // 2) * RANK
            low = low_ref[row : row + SEG, col : col + RANK].astype(jnp.bfloat16)
            up = jnp.dot(low, mats_ref[pick_ref[k]], preferred_element_type=jnp.float32)
            acc_ref[k * SEG : (k + 1) * SEG, :] = 2.0 * up
        acc_ref[...] += part

    @pl.when(step > 0)
    def _():
        acc_ref[...] += part

    @pl.when(step == pl.num_programs(0) - 1)
    def _():
        out_ref[...] = acc_ref[...].astype(jnp.bfloat16)


def main_product(pick, low, mats, gathered, weight, own_half):
    depth = 1024
    per_half = 4096 // depth

    def t_index(i, pick):
        return (i // per_half, i % per_half)

    def w_index(i, pick):
        half = jnp.where(i < per_half, pick[4], 1 - pick[4])
        return (half * per_half + i % per_half, 0)

    grid_spec = pltpu.PrefetchScalarGridSpec(
        num_scalar_prefetch=1,
        grid=(2 * per_half,),
        in_specs=[
            pl.BlockSpec((256, 128), lambda i, pick: (0, 0)),
            pl.BlockSpec(mats.shape, lambda i, pick: (0, 0, 0)),
            pl.BlockSpec((ROWS, depth), t_index),
            pl.BlockSpec((depth, WIDTH), w_index),
        ],
        out_specs=pl.BlockSpec((ROWS, WIDTH), lambda i, pick: (0, 0)),
        scratch_shapes=[pltpu.VMEM((ROWS, WIDTH), jnp.float32)],
    )
    return pl.pallas_call(
        main_kernel,
        out_shape=jax.ShapeDtypeStruct((ROWS, WIDTH), jnp.bfloat16),
        grid_spec=grid_spec,
        compiler_params=pltpu.CompilerParams(vmem_limit_bytes=40 << 20),
        cost_estimate=pl.CostEstimate(
            flops=2 * ROWS * 8192 * WIDTH, bytes_accessed=12 << 20, transcendentals=0
        ),
    )(jnp.concatenate([pick, own_half[None]]), low, mats, gathered, weight)


def body(tokens, weight, down, up, segment_request, request_ids, stored_row):
    dp = lax.axis_index(DP).astype(jnp.int32)
    half = lax.axis_index("xl").astype(jnp.int32)

    other = lax.ppermute(tokens, "xl", SWAP)
    gathered = lax.all_gather(
        jnp.concatenate([tokens, other], axis=0), ("y", "c"), axis=1, tiled=True
    )

    hits = request_ids[:, None] == jnp.arange(stored_row.shape[0], dtype=jnp.int32)[None, :]
    rows = jnp.sum(jnp.where(hits, stored_row[None, :], 0), axis=1).astype(jnp.int32)
    every_row = lax.all_to_all(
        jnp.broadcast_to(rows[None, None, :], (16, 1, 2)), DP, 0, 0
    ).reshape(32)
    request = segment_request - dp * 2
    owner_slot = (rows // OWNED) * 2 + jnp.arange(2, dtype=jnp.int32)
    pick = jnp.where(request == 0, owner_slot[0], owner_slot[1]).astype(jnp.int32)

    me = dp[None]
    sent_down = select(every_row, me, down)
    sent_up = select(every_row, me, up)
    got_down = lax.all_to_all(sent_down.reshape(16, 2, RANK, WIDTH), DP, 0, 0)
    got_up = lax.all_to_all(sent_up.reshape(16, 2, RANK, WIDTH), DP, 0, 0)

    partial = down_product(pick, tokens, got_down.reshape(32, RANK, WIDTH))
    parts = lax.all_to_all(partial.reshape(32, 8, 128), TENSOR, 0, 0)
    total = jnp.sum(parts, axis=0)
    low = lax.all_to_all(jnp.broadcast_to(total[None], (32, 8, 128)), TENSOR, 0, 0)
    return main_product(
        pick, low.reshape(256, 128), got_up.reshape(32, RANK, WIDTH), gathered, weight, half
    )


def solution(mesh):
    fine = Mesh(mesh.devices.reshape(2, 8, 2, 8, 2), ("xh", "z", "xl", "y", "c"))
    in_specs = (
        P(DP, TENSOR),
        P(None, TENSOR),
        P(DP, None, TENSOR),
        P(DP, None, TENSOR),
        P(DP),
        P(DP),
        P(),
    )
    return jax.shard_map(body, mesh=fine, in_specs=in_specs, out_specs=P(DP, TENSOR), check_vma=False)
```

```python
import jax
import jax.numpy as jnp
from jax import lax
from jax.experimental import pallas as pl
from jax.experimental.pallas import tpu as pltpu
from jax.sharding import Mesh, PartitionSpec as P

SWAP = [(0, 1), (1, 0)]
DP = ("xh", "z")
X = ("xh", "xl")
TENSOR = ("xl", "y", "c")
ROWS = 512
SEG = 128
RANK = 64
WIDTH = 256
OWNED = 4
ZS = 8
HALF = 4096
DEPTH = 1024

ANY = pl.BlockSpec(memory_space=pl.ANY)
SMEM = pl.BlockSpec(memory_space=pltpu.SMEM)
VMEM = pl.BlockSpec(memory_space=pltpu.VMEM)


def select_kernel(ids_ref, stored_ref, xh_ref, down_ref, up_ref, other_ref, out_ref, sems):
    copies = []
    for z in range(ZS):
        for r in range(2):
            row = stored_ref[ids_ref[z, r]]
            slot = row % OWNED
            mine = row // (OWNED * ZS) == xh_ref[0]
            for part, own in enumerate((down_ref, up_ref)):
                sem = sems.at[z, r, part]
                target = out_ref.at[z, 2 * r + part]

                @pl.when(mine)
                def _():
                    pltpu.make_async_copy(own.at[slot], target, sem).start()

                @pl.when(jnp.logical_not(mine))
                def _():
                    pltpu.make_async_copy(other_ref.at[part, slot], target, sem).start()

                copies.append(pltpu.make_async_copy(own.at[0], target, sem))
    for copy in copies:
        copy.wait()


def select(ids, stored, xh, down, up, other):
    return pl.pallas_call(
        select_kernel,
        out_shape=jax.ShapeDtypeStruct((ZS, 4, RANK, WIDTH), down.dtype),
        in_specs=[SMEM, SMEM, SMEM, ANY, ANY, ANY],
        out_specs=ANY,
        scratch_shapes=[pltpu.SemaphoreType.DMA((ZS, 2, 2))],
        cost_estimate=pl.CostEstimate(flops=0, bytes_accessed=2 << 20, transcendentals=0),
    )(ids, stored, xh, down, up, other)


def fetch(ids_ref, stored_ref, got_ref, mats, sems, part):
    copies = []
    for r in range(2):
        source = stored_ref[ids_ref[r]] // OWNED % ZS
        copy = pltpu.make_async_copy(got_ref.at[source, 2 * r + part], mats.at[r], sems.at[r])
        copy.start()
        copies.append(copy)
    return copies


def down_kernel(ids_ref, stored_ref, seg_ref, dp_ref, tokens_ref, got_ref, out_ref, mats, sems):
    for copy in fetch(ids_ref, stored_ref, got_ref, mats, sems, 0):
        copy.wait()
    for k in range(4):
        part = lax.dot_general(
            tokens_ref[k * SEG : (k + 1) * SEG, :],
            mats[seg_ref[k] - 2 * dp_ref[0]],
            (((1,), (1,)), ((), ())),
            preferred_element_type=jnp.float32,
        )
        row, col = (k % 2) * SEG, (k // 2) * RANK
        out_ref[row : row + SEG, col : col + RANK] = part


def down_product(ids, stored, seg, dp, tokens, got):
    return pl.pallas_call(
        down_kernel,
        out_shape=jax.ShapeDtypeStruct((256, 128), jnp.float32),
        in_specs=[SMEM, SMEM, SMEM, SMEM, VMEM, ANY],
        out_specs=VMEM,
        scratch_shapes=[
            pltpu.VMEM((2, RANK, WIDTH), jnp.bfloat16),
            pltpu.SemaphoreType.DMA((2,)),
        ],
        cost_estimate=pl.CostEstimate(flops=1 << 24, bytes_accessed=1 << 20, transcendentals=0),
    )(ids, stored, seg, dp, tokens, got)


def base_kernel(half_ref, t_ref, wa_ref, wb_ref, w_ref, theirs_ref, ours_ref):
    step = pl.program_id(0)
    t = t_ref[...]

    @pl.when(step == 0)
    def _():
        theirs_ref[...] = jnp.zeros_like(theirs_ref)
        ours_ref[...] = jnp.zeros_like(ours_ref)

    @pl.when(step < 2)
    def _():
        theirs_ref[...] += jnp.dot(t, wa_ref[...], preferred_element_type=jnp.float32)

    @pl.when(step >= 2)
    def _():
        theirs_ref[...] += jnp.dot(t, wb_ref[...], preferred_element_type=jnp.float32)

    ours_ref[...] += jnp.dot(t, w_ref[...], preferred_element_type=jnp.float32)


def base_products(half, gathered, wa, wb, weight):
    steps = HALF // DEPTH
    whole = pl.BlockSpec((ROWS, WIDTH), lambda i, half: (0, 0))
    grid_spec = pltpu.PrefetchScalarGridSpec(
        num_scalar_prefetch=1,
        grid=(steps,),
        in_specs=[
            pl.BlockSpec((ROWS, DEPTH), lambda i, half: (0, i)),
            pl.BlockSpec((DEPTH, WIDTH), lambda i, half: (jnp.minimum(i, 1), 0)),
            pl.BlockSpec((DEPTH, WIDTH), lambda i, half: (jnp.maximum(i - 2, 0), 0)),
            pl.BlockSpec((DEPTH, WIDTH), lambda i, half: (half[0] * steps + i, 0)),
        ],
        out_specs=[whole, whole],
    )
    shape = jax.ShapeDtypeStruct((ROWS, WIDTH), jnp.float32)
    return pl.pallas_call(
        base_kernel,
        out_shape=[shape, shape],
        grid_spec=grid_spec,
        cost_estimate=pl.CostEstimate(
            flops=4 * ROWS * HALF * WIDTH, bytes_accessed=10 << 20, transcendentals=0
        ),
    )(half, gathered, wa, wb, weight)


def last_kernel(
    ids_ref, stored_ref, seg_ref, dp_ref, low_ref, got_ref, ours_ref, recv_ref, out_ref, mats, sems
):
    copies = fetch(ids_ref, stored_ref, got_ref, mats, sems, 1)
    for copy in copies:
        copy.wait()
    for k in range(4):
        row, col = (k % 2) * SEG, (k // 2) * RANK
        low = low_ref[row : row + SEG, col : col + RANK].astype(jnp.bfloat16)
        up = jnp.dot(low, mats[seg_ref[k] - 2 * dp_ref[0]], preferred_element_type=jnp.float32)
        rows = slice(k * SEG, (k + 1) * SEG)
        out_ref[rows, :] = (ours_ref[rows, :] + recv_ref[rows, :] + 2.0 * up).astype(jnp.bfloat16)


def last_product(ids, stored, seg, dp, low, got, ours, recv):
    return pl.pallas_call(
        last_kernel,
        out_shape=jax.ShapeDtypeStruct((ROWS, WIDTH), jnp.bfloat16),
        in_specs=[SMEM, SMEM, SMEM, SMEM, VMEM, ANY, VMEM, VMEM],
        out_specs=VMEM,
        scratch_shapes=[
            pltpu.VMEM((2, RANK, WIDTH), jnp.bfloat16),
            pltpu.SemaphoreType.DMA((2,)),
        ],
        cost_estimate=pl.CostEstimate(flops=1 << 24, bytes_accessed=2 << 20, transcendentals=0),
    )(ids, stored, seg, dp, low, got, ours, recv)


def body(tokens, weight, down, up, segment_request, request_ids, stored_row):
    xh = lax.axis_index("xh").astype(jnp.int32)
    xl = lax.axis_index("xl").astype(jnp.int32)
    dp = lax.axis_index(DP).astype(jnp.int32)[None]

    gathered = lax.all_gather(tokens, ("y", "c"), axis=1, tiled=True)

    every_id = lax.all_to_all(
        jnp.broadcast_to(request_ids[None, :], (ZS, 2)), "z", 0, 0, tiled=True
    )
    other = lax.ppermute(jnp.stack([down, up]), "xh", SWAP)

    quarter = HALF // 2
    start = (1 - xl) * HALF
    wa = lax.ppermute(
        lax.dynamic_slice_in_dim(weight, start, quarter, 0), X, [(i, (i + 1) % 4) for i in range(4)]
    )
    wb = lax.ppermute(
        lax.dynamic_slice_in_dim(weight, start + quarter, quarter, 0),
        X,
        [(i, (i + 3) % 4) for i in range(4)],
    )

    sent = select(every_id, stored_row, xh[None], down, up, other)
    got = lax.all_to_all(sent, "z", 0, 0, tiled=True)

    partial = down_product(request_ids, stored_row, segment_request, dp, tokens, got)
    parts = lax.all_to_all(partial.reshape(32, 8, 128), TENSOR, 0, 0)
    total = jnp.sum(parts, axis=0)
    low = lax.all_to_all(jnp.broadcast_to(total[None], (32, 8, 128)), TENSOR, 0, 0)

    theirs, ours = base_products(xl[None], gathered, wa, wb, weight)
    recv = lax.ppermute(theirs, "xl", SWAP)
    return last_product(
        request_ids, stored_row, segment_request, dp, low.reshape(256, 128), got, ours, recv
    )


def solution(mesh):
    fine = Mesh(mesh.devices.reshape(2, 8, 2, 8, 2), ("xh", "z", "xl", "y", "c"))
    in_specs = (
        P(DP, TENSOR),
        P(None, TENSOR),
        P(DP, None, TENSOR),
        P(DP, None, TENSOR),
        P(DP),
        P(DP),
        P(),
    )
    return jax.shard_map(body, mesh=fine, in_specs=in_specs, out_specs=P(DP, TENSOR), check_vma=False)
```

```python
import jax
import jax.numpy as jnp
from jax import lax
from jax.experimental import pallas as pl
from jax.experimental.pallas import tpu as pltpu
from jax.sharding import Mesh, PartitionSpec as P

SWAP = [(0, 1), (1, 0)]
DP = ("xh", "z")
X = ("xh", "xl")
TENSOR = ("xl", "y", "c")
ROWS = 512
SEG = 128
RANK = 64
WIDTH = 256
OWNED = 4
ZS = 8
HALF = 4096
DEPTH = 1024

ANY = pl.BlockSpec(memory_space=pl.ANY)
SMEM = pl.BlockSpec(memory_space=pltpu.SMEM)
VMEM = pl.BlockSpec(memory_space=pltpu.VMEM)


def select_kernel(ids_ref, stored_ref, xh_ref, own_ref, other_ref, out_ref):
    def step(i, carry):
        z, r = i // 2, i % 2
        row = stored_ref[ids_ref[z, r]]
        slot = row % OWNED
        mine = row // (OWNED * ZS) == xh_ref[0]

        @pl.when(mine)
        def _():
            for part in range(2):
                out_ref[z, 2 * r + part] = own_ref[part, slot]

        @pl.when(jnp.logical_not(mine))
        def _():
            for part in range(2):
                out_ref[z, 2 * r + part] = other_ref[part, slot]

        return carry

    lax.fori_loop(0, 2 * ZS, step, 0)


def select(ids, stored, xh, own, other):
    return pl.pallas_call(
        select_kernel,
        out_shape=jax.ShapeDtypeStruct((ZS, 4, RANK, WIDTH), own.dtype),
        in_specs=[SMEM, SMEM, SMEM, VMEM, VMEM],
        out_specs=VMEM,
        cost_estimate=pl.CostEstimate(flops=0, bytes_accessed=2 << 20, transcendentals=0),
    )(ids, stored, xh, own, other)


def fetch(ids_ref, stored_ref, got_ref, mats, sems, part):
    copies = []
    for r in range(2):
        source = stored_ref[ids_ref[r]] // OWNED % ZS
        copy = pltpu.make_async_copy(got_ref.at[source, 2 * r + part], mats.at[r], sems.at[r])
        copy.start()
        copies.append(copy)
    return copies


def down_kernel(ids_ref, stored_ref, seg_ref, dp_ref, tokens_ref, got_ref, out_ref, mats, sems):
    for copy in fetch(ids_ref, stored_ref, got_ref, mats, sems, 0):
        copy.wait()
    for k in range(4):
        part = lax.dot_general(
            tokens_ref[k * SEG : (k + 1) * SEG, :],
            mats[seg_ref[k] - 2 * dp_ref[0]],
            (((1,), (1,)), ((), ())),
            preferred_element_type=jnp.float32,
        )
        row, col = (k % 2) * SEG, (k // 2) * RANK
        out_ref[row : row + SEG, col : col + RANK] = part


def down_product(ids, stored, seg, dp, tokens, got):
    return pl.pallas_call(
        down_kernel,
        out_shape=jax.ShapeDtypeStruct((256, 128), jnp.float32),
        in_specs=[SMEM, SMEM, SMEM, SMEM, VMEM, ANY],
        out_specs=VMEM,
        scratch_shapes=[
            pltpu.VMEM((2, RANK, WIDTH), jnp.bfloat16),
            pltpu.SemaphoreType.DMA((2,)),
        ],
        cost_estimate=pl.CostEstimate(flops=1 << 24, bytes_accessed=1 << 20, transcendentals=0),
    )(ids, stored, seg, dp, tokens, got)


def base_kernel(half_ref, t_ref, wa_ref, wb_ref, w_ref, theirs_ref, ours_ref, t, wt, wo, sems):
    count = HALF // DEPTH
    per_quarter = count // 2
    copies = []
    for i in range(count):
        cols = slice(i * DEPTH, (i + 1) * DEPTH)
        source = wa_ref if i < per_quarter else wb_ref
        rows = pl.ds((i % per_quarter) * DEPTH, DEPTH)
        start = pl.multiple_of(half_ref[0] * HALF + i * DEPTH, DEPTH)
        trio = (
            pltpu.make_async_copy(t_ref.at[:, cols], t.at[i], sems.at[i, 0]),
            pltpu.make_async_copy(source.at[rows, :], wt.at[i], sems.at[i, 1]),
            pltpu.make_async_copy(w_ref.at[pl.ds(start, DEPTH), :], wo.at[i], sems.at[i, 2]),
        )
        for copy in trio:
            copy.start()
        copies.append(trio)
    for i in range(count):
        for copy in copies[i]:
            copy.wait()
        theirs = jnp.dot(t[i], wt[i], preferred_element_type=jnp.float32)
        ours = jnp.dot(t[i], wo[i], preferred_element_type=jnp.float32)
        if i == 0:
            theirs_ref[...] = theirs
            ours_ref[...] = ours
        else:
            theirs_ref[...] += theirs
            ours_ref[...] += ours


def base_products(half, gathered, wa, wb, weight):
    count = HALF // DEPTH
    shape = jax.ShapeDtypeStruct((ROWS, WIDTH), jnp.float32)
    return pl.pallas_call(
        base_kernel,
        out_shape=[shape, shape],
        in_specs=[SMEM, ANY, ANY, ANY, ANY],
        out_specs=[VMEM, VMEM],
        scratch_shapes=[
            pltpu.VMEM((count, ROWS, DEPTH), jnp.bfloat16),
            pltpu.VMEM((count, DEPTH, WIDTH), jnp.bfloat16),
            pltpu.VMEM((count, DEPTH, WIDTH), jnp.bfloat16),
            pltpu.SemaphoreType.DMA((count, 3)),
        ],
        cost_estimate=pl.CostEstimate(
            flops=4 * ROWS * HALF * WIDTH, bytes_accessed=10 << 20, transcendentals=0
        ),
    )(half, gathered, wa, wb, weight)


def last_kernel(
    ids_ref, stored_ref, seg_ref, dp_ref, low_ref, got_ref, ours_ref, recv_ref, out_ref, mats, sems
):
    copies = fetch(ids_ref, stored_ref, got_ref, mats, sems, 1)
    for copy in copies:
        copy.wait()
    for k in range(4):
        row, col = (k % 2) * SEG, (k // 2) * RANK
        low = low_ref[row : row + SEG, col : col + RANK]
        up = jnp.dot(low, mats[seg_ref[k] - 2 * dp_ref[0]], preferred_element_type=jnp.float32)
        rows = slice(k * SEG, (k + 1) * SEG)
        out_ref[rows, :] = (ours_ref[rows, :] + recv_ref[rows, :] + 2.0 * up).astype(jnp.bfloat16)


def last_product(ids, stored, seg, dp, low, got, ours, recv):
    return pl.pallas_call(
        last_kernel,
        out_shape=jax.ShapeDtypeStruct((ROWS, WIDTH), jnp.bfloat16),
        in_specs=[SMEM, SMEM, SMEM, SMEM, VMEM, ANY, VMEM, VMEM],
        out_specs=VMEM,
        scratch_shapes=[
            pltpu.VMEM((2, RANK, WIDTH), jnp.bfloat16),
            pltpu.SemaphoreType.DMA((2,)),
        ],
        cost_estimate=pl.CostEstimate(flops=1 << 24, bytes_accessed=2 << 20, transcendentals=0),
    )(ids, stored, seg, dp, low, got, ours, recv)


def body(tokens, weight, down, up, segment_request, request_ids, stored_row):
    xh = lax.axis_index("xh").astype(jnp.int32)
    xl = lax.axis_index("xl").astype(jnp.int32)
    dp = lax.axis_index(DP).astype(jnp.int32)[None]

    gathered = lax.all_gather(tokens, ("y", "c"), axis=1, tiled=True)

    every_id = lax.all_to_all(
        jnp.broadcast_to(request_ids[None, :], (ZS, 2)), "z", 0, 0, tiled=True
    )
    own = jnp.stack([down, up])
    other = lax.ppermute(own, "xh", SWAP)

    quarter = HALF // 2
    start = (1 - xl) * HALF
    wa = lax.ppermute(
        lax.dynamic_slice_in_dim(weight, start, quarter, 0), X, [(i, (i + 1) % 4) for i in range(4)]
    )
    wb = lax.ppermute(
        lax.dynamic_slice_in_dim(weight, start + quarter, quarter, 0),
        X,
        [(i, (i + 3) % 4) for i in range(4)],
    )

    sent = select(every_id, stored_row, xh[None], own, other)
    got = lax.all_to_all(sent, "z", 0, 0, tiled=True)
    got, _, _ = lax.optimization_barrier((got, wa, wb))

    partial = down_product(request_ids, stored_row, segment_request, dp, tokens, got)
    parts = lax.all_to_all(partial.reshape(32, 8, 128), TENSOR, 0, 0)
    total = jnp.sum(parts, axis=0).astype(jnp.bfloat16)
    low = lax.all_to_all(jnp.broadcast_to(total[None], (32, 8, 128)), TENSOR, 0, 0)

    weight, _ = lax.optimization_barrier((weight, partial))
    theirs, ours = base_products(xl[None], gathered, wa, wb, weight)
    recv = lax.ppermute(theirs, "xl", SWAP)
    return last_product(
        request_ids, stored_row, segment_request, dp, low.reshape(256, 128), got, ours, recv
    )


def solution(mesh):
    fine = Mesh(mesh.devices.reshape(2, 8, 2, 8, 2), ("xh", "z", "xl", "y", "c"))
    in_specs = (
        P(DP, TENSOR),
        P(None, TENSOR),
        P(DP, None, TENSOR),
        P(DP, None, TENSOR),
        P(DP),
        P(DP),
        P(),
    )
    return jax.shard_map(body, mesh=fine, in_specs=in_specs, out_specs=P(DP, TENSOR), check_vma=False)
```

```python
import jax
import jax.numpy as jnp
from jax import lax
from jax.experimental import pallas as pl
from jax.experimental.pallas import tpu as pltpu
from jax.sharding import Mesh, PartitionSpec as P

SWAP = [(0, 1), (1, 0)]
DP = ("xh", "zh", "zl")
X = ("xh", "xl")
TENSOR = ("xl", "y", "c")
ROWS = 512
SEG = 128
RANK = 64
WIDTH = 256
OWNED = 4
ZS = 8
PEERS = 4
HALF = 4096
DEPTH = 1024

ANY = pl.BlockSpec(memory_space=pl.ANY)
SMEM = pl.BlockSpec(memory_space=pltpu.SMEM)
VMEM = pl.BlockSpec(memory_space=pltpu.VMEM)


def vmem(mib):
    return pltpu.CompilerParams(vmem_limit_bytes=mib << 20)


def select_kernel(ids_ref, stored_ref, place_ref, own_ref, x_ref, z_ref, xz_ref, out_ref):
    held = (own_ref, x_ref, z_ref, xz_ref)

    def step(i, carry):
        zh, r = i // 2, i % 2
        row = stored_ref[ids_ref[zh, 0, r]]
        slot = row % OWNED
        owner = row // OWNED
        across_x = owner // ZS != place_ref[0]
        across_z = owner % 2 != place_ref[1]
        which = across_x.astype(jnp.int32) + 2 * across_z.astype(jnp.int32)
        for j in range(4):

            @pl.when(which == j)
            def _():
                for part in range(2):
                    out_ref[zh, 2 * r + part] = held[j][part, slot]

        return carry

    lax.fori_loop(0, 2 * PEERS, step, 0)


def select(ids, stored, place, own, x, z, xz):
    return pl.pallas_call(
        select_kernel,
        out_shape=jax.ShapeDtypeStruct((PEERS, 4, RANK, WIDTH), own.dtype),
        in_specs=[SMEM, SMEM, SMEM, VMEM, VMEM, VMEM, VMEM],
        out_specs=VMEM,
        compiler_params=vmem(8),
        cost_estimate=pl.CostEstimate(flops=0, bytes_accessed=2 << 20, transcendentals=0),
    )(ids, stored, place, own, x, z, xz)


def fetch(ids_ref, stored_ref, got_ref, mats, sems, part):
    copies = []
    for r in range(2):
        source = stored_ref[ids_ref[r]] // OWNED % ZS // 2
        copy = pltpu.make_async_copy(got_ref.at[source, 2 * r + part], mats.at[r], sems.at[r])
        copy.start()
        copies.append(copy)
    return copies


def down_kernel(ids_ref, stored_ref, seg_ref, dp_ref, tokens_ref, got_ref, out_ref, mats, sems):
    for copy in fetch(ids_ref, stored_ref, got_ref, mats, sems, 0):
        copy.wait()
    for k in range(4):
        part = lax.dot_general(
            tokens_ref[k * SEG : (k + 1) * SEG, :],
            mats[seg_ref[k] - 2 * dp_ref[0]],
            (((1,), (1,)), ((), ())),
            preferred_element_type=jnp.float32,
        )
        row, col = (k % 2) * SEG, (k // 2) * RANK
        out_ref[row : row + SEG, col : col + RANK] = part


def down_product(ids, stored, seg, dp, tokens, got):
    return pl.pallas_call(
        down_kernel,
        out_shape=jax.ShapeDtypeStruct((256, 128), jnp.float32),
        in_specs=[SMEM, SMEM, SMEM, SMEM, VMEM, ANY],
        out_specs=VMEM,
        scratch_shapes=[
            pltpu.VMEM((2, RANK, WIDTH), jnp.bfloat16),
            pltpu.SemaphoreType.DMA((2,)),
        ],
        compiler_params=vmem(4),
        cost_estimate=pl.CostEstimate(flops=1 << 24, bytes_accessed=1 << 20, transcendentals=0),
    )(ids, stored, seg, dp, tokens, got)


def sum_kernel(parts_ref, out_ref):
    total = jnp.sum(parts_ref[...], axis=0).astype(jnp.bfloat16)
    out_ref[...] = jnp.broadcast_to(total[None], out_ref.shape)


def sum_parts(parts):
    return pl.pallas_call(
        sum_kernel,
        out_shape=jax.ShapeDtypeStruct(parts.shape, jnp.bfloat16),
        in_specs=[VMEM],
        out_specs=VMEM,
        compiler_params=vmem(4),
        cost_estimate=pl.CostEstimate(flops=0, bytes_accessed=128 << 20, transcendentals=0),
    )(parts)


def base_kernel(half_ref, t_ref, wa_ref, wb_ref, w_ref, theirs_ref, ours_ref, t, wt, wo, acc, sems):
    count = HALF // DEPTH
    per_quarter = count // 2
    copies = []
    for i in range(count):
        cols = slice(i * DEPTH, (i + 1) * DEPTH)
        source = wa_ref if i < per_quarter else wb_ref
        rows = pl.ds((i % per_quarter) * DEPTH, DEPTH)
        start = pl.multiple_of(half_ref[0] * HALF + i * DEPTH, DEPTH)
        trio = (
            pltpu.make_async_copy(t_ref.at[:, cols], t.at[i], sems.at[i, 0]),
            pltpu.make_async_copy(source.at[rows, :], wt.at[i], sems.at[i, 1]),
            pltpu.make_async_copy(w_ref.at[pl.ds(start, DEPTH), :], wo.at[i], sems.at[i, 2]),
        )
        for copy in trio:
            copy.start()
        copies.append(trio)
    for i in range(count):
        for copy in copies[i]:
            copy.wait()
        theirs = jnp.dot(t[i], wt[i], preferred_element_type=jnp.float32)
        ours = jnp.dot(t[i], wo[i], preferred_element_type=jnp.float32)
        if i == 0:
            acc[...] = theirs
            ours_ref[...] = ours
        else:
            acc[...] += theirs
            ours_ref[...] += ours
    theirs_ref[...] = acc[...].astype(jnp.bfloat16)


def base_products(half, gathered, wa, wb, weight):
    count = HALF // DEPTH
    return pl.pallas_call(
        base_kernel,
        out_shape=[
            jax.ShapeDtypeStruct((ROWS, WIDTH), jnp.bfloat16),
            jax.ShapeDtypeStruct((ROWS, WIDTH), jnp.float32),
        ],
        in_specs=[SMEM, ANY, ANY, ANY, ANY],
        out_specs=[VMEM, VMEM],
        scratch_shapes=[
            pltpu.VMEM((count, ROWS, DEPTH), jnp.bfloat16),
            pltpu.VMEM((count, DEPTH, WIDTH), jnp.bfloat16),
            pltpu.VMEM((count, DEPTH, WIDTH), jnp.bfloat16),
            pltpu.VMEM((ROWS, WIDTH), jnp.float32),
            pltpu.SemaphoreType.DMA((count, 3)),
        ],
        compiler_params=vmem(56),
        cost_estimate=pl.CostEstimate(
            flops=4 * ROWS * HALF * WIDTH, bytes_accessed=10 << 20, transcendentals=0
        ),
    )(half, gathered, wa, wb, weight)


def last_kernel(
    ids_ref, stored_ref, seg_ref, dp_ref, low_ref, got_ref, ours_ref, recv_ref, out_ref, mats, sems
):
    copies = fetch(ids_ref, stored_ref, got_ref, mats, sems, 1)
    for copy in copies:
        copy.wait()
    for k in range(4):
        row, col = (k % 2) * SEG, (k // 2) * RANK
        low = low_ref[row : row + SEG, col : col + RANK]
        up = jnp.dot(low, mats[seg_ref[k] - 2 * dp_ref[0]], preferred_element_type=jnp.float32)
        rows = slice(k * SEG, (k + 1) * SEG)
        out_ref[rows, :] = (ours_ref[rows, :] + recv_ref[rows, :].astype(jnp.float32) + 2.0 * up).astype(jnp.bfloat16)


def last_product(ids, stored, seg, dp, low, got, ours, recv):
    return pl.pallas_call(
        last_kernel,
        out_shape=jax.ShapeDtypeStruct((ROWS, WIDTH), jnp.bfloat16),
        in_specs=[SMEM, SMEM, SMEM, SMEM, VMEM, ANY, VMEM, VMEM],
        out_specs=VMEM,
        scratch_shapes=[
            pltpu.VMEM((2, RANK, WIDTH), jnp.bfloat16),
            pltpu.SemaphoreType.DMA((2,)),
        ],
        compiler_params=vmem(8),
        cost_estimate=pl.CostEstimate(flops=1 << 24, bytes_accessed=2 << 20, transcendentals=0),
    )(ids, stored, seg, dp, low, got, ours, recv)


def body(tokens, weight, down, up, segment_request, request_ids, stored_row):
    xl = lax.axis_index("xl").astype(jnp.int32)
    dp = lax.axis_index(DP).astype(jnp.int32)[None]
    place = jnp.stack([lax.axis_index("xh"), lax.axis_index("zl")]).astype(jnp.int32)

    gathered = lax.all_gather(tokens, ("y", "c"), axis=1, tiled=True)

    every_id = lax.all_to_all(
        jnp.broadcast_to(request_ids[None, None, :], (PEERS, 1, 2)), "zh", 0, 0, tiled=True
    )
    own = jnp.stack([down, up])
    pair = ("xh", "zl")
    far = [lax.ppermute(own, pair, [(i, i ^ flip) for i in range(4)]) for flip in (2, 1, 3)]

    sent = select(every_id, stored_row, place, own, *far)
    late_weight, _ = lax.optimization_barrier((weight, every_id))
    quarter = HALF // 2
    start = (1 - xl) * HALF
    wa = lax.ppermute(
        lax.dynamic_slice_in_dim(late_weight, start, quarter, 0), X, [(i, (i + 1) % 4) for i in range(4)]
    )
    wb = lax.ppermute(
        lax.dynamic_slice_in_dim(late_weight, start + quarter, quarter, 0),
        X,
        [(i, (i + 3) % 4) for i in range(4)],
    )

    got = lax.all_to_all(sent, "zh", 0, 0, tiled=True)

    partial = down_product(request_ids, stored_row, segment_request, dp, tokens, got)
    parts = lax.all_to_all(partial.reshape(32, 8, 128), TENSOR, 0, 0)
    low = lax.all_to_all(sum_parts(parts), TENSOR, 0, 0)

    weight, _ = lax.optimization_barrier((weight, partial))
    theirs, ours = base_products(xl[None], gathered, wa, wb, weight)
    recv = lax.ppermute(theirs, "xl", SWAP)
    return last_product(
        request_ids, stored_row, segment_request, dp, low.reshape(256, 128), got, ours, recv
    )


def solution(mesh):
    fine = Mesh(mesh.devices.reshape(2, 4, 2, 2, 8, 2), ("xh", "zh", "zl", "xl", "y", "c"))
    in_specs = (
        P(DP, TENSOR),
        P(None, TENSOR),
        P(DP, None, TENSOR),
        P(DP, None, TENSOR),
        P(DP),
        P(DP),
        P(),
    )
    return jax.shard_map(body, mesh=fine, in_specs=in_specs, out_specs=P(DP, TENSOR), check_vma=False)
```

```python
import jax
import jax.numpy as jnp
from jax import lax
from jax.experimental import pallas as pl
from jax.experimental.pallas import tpu as pltpu
from jax.sharding import Mesh, PartitionSpec as P

SWAP = [(0, 1), (1, 0)]
DP = ("xh", "zh", "zl")
X = ("xh", "xl")
TENSOR = ("xl", "y", "c")
ROWS = 512
SEG = 128
RANK = 64
WIDTH = 256
OWNED = 4
ZS = 8
PEERS = 4
HALF = 4096
DEPTH = 1024

ANY = pl.BlockSpec(memory_space=pl.ANY)
SMEM = pl.BlockSpec(memory_space=pltpu.SMEM)
VMEM = pl.BlockSpec(memory_space=pltpu.VMEM)


def vmem(mib):
    return pltpu.CompilerParams(vmem_limit_bytes=mib << 20)


def select_kernel(ids_ref, stored_ref, place_ref, own_ref, x_ref, z_ref, xz_ref, out_ref):
    held = (own_ref, x_ref, z_ref, xz_ref)

    def step(i, carry):
        zh, r = i // 2, i % 2
        row = stored_ref[ids_ref[zh, 0, r]]
        slot = row % OWNED
        owner = row // OWNED
        across_x = owner // ZS != place_ref[0]
        across_z = owner % 2 != place_ref[1]
        which = across_x.astype(jnp.int32) + 2 * across_z.astype(jnp.int32)
        for j in range(4):

            @pl.when(which == j)
            def _():
                for part in range(2):
                    out_ref[zh, 2 * r + part] = held[j][part, slot]

        return carry

    lax.fori_loop(0, 2 * PEERS, step, 0)


def select(ids, stored, place, own, x, z, xz):
    return pl.pallas_call(
        select_kernel,
        out_shape=jax.ShapeDtypeStruct((PEERS, 4, RANK, WIDTH), own.dtype),
        in_specs=[SMEM, SMEM, SMEM, VMEM, VMEM, VMEM, VMEM],
        out_specs=VMEM,
        compiler_params=vmem(8),
        cost_estimate=pl.CostEstimate(flops=0, bytes_accessed=2 << 20, transcendentals=0),
    )(ids, stored, place, own, x, z, xz)


def fetch(ids_ref, stored_ref, got_ref, mats, sems, part):
    copies = []
    for r in range(2):
        source = stored_ref[ids_ref[r]] // OWNED % ZS // 2
        copy = pltpu.make_async_copy(got_ref.at[source, 2 * r + part], mats.at[r], sems.at[r])
        copy.start()
        copies.append(copy)
    return copies


def down_kernel(ids_ref, stored_ref, seg_ref, dp_ref, tokens_ref, got_ref, out_ref, mats, sems):
    for copy in fetch(ids_ref, stored_ref, got_ref, mats, sems, 0):
        copy.wait()
    for k in range(4):
        part = lax.dot_general(
            tokens_ref[k * SEG : (k + 1) * SEG, :],
            mats[seg_ref[k] - 2 * dp_ref[0]],
            (((1,), (1,)), ((), ())),
            preferred_element_type=jnp.float32,
        )
        row, col = (k % 2) * SEG, (k // 2) * RANK
        out_ref[row : row + SEG, col : col + RANK] = part


def down_product(ids, stored, seg, dp, tokens, got):
    return pl.pallas_call(
        down_kernel,
        out_shape=jax.ShapeDtypeStruct((256, 128), jnp.float32),
        in_specs=[SMEM, SMEM, SMEM, SMEM, VMEM, ANY],
        out_specs=VMEM,
        scratch_shapes=[
            pltpu.VMEM((2, RANK, WIDTH), jnp.bfloat16),
            pltpu.SemaphoreType.DMA((2,)),
        ],
        compiler_params=vmem(4),
        cost_estimate=pl.CostEstimate(flops=1 << 24, bytes_accessed=1 << 20, transcendentals=0),
    )(ids, stored, seg, dp, tokens, got)


def sum_kernel(parts_ref, out_ref):
    total = jnp.sum(parts_ref[...], axis=0).astype(jnp.bfloat16)
    out_ref[...] = jnp.broadcast_to(total[None], out_ref.shape)


def sum_parts(parts):
    return pl.pallas_call(
        sum_kernel,
        out_shape=jax.ShapeDtypeStruct(parts.shape, jnp.bfloat16),
        in_specs=[VMEM],
        out_specs=VMEM,
        compiler_params=vmem(4),
        cost_estimate=pl.CostEstimate(flops=0, bytes_accessed=128 << 20, transcendentals=0),
    )(parts)


def base_kernel(half_ref, t_ref, wa_ref, wb_ref, w_ref, theirs_ref, ours_ref, t, wt, wo, acc, sems):
    count = HALF // DEPTH
    per_quarter = count // 2
    copies = []
    for i in range(count):
        cols = slice(i * DEPTH, (i + 1) * DEPTH)
        source = wa_ref if i < per_quarter else wb_ref
        rows = pl.ds((i % per_quarter) * DEPTH, DEPTH)
        start = pl.multiple_of(half_ref[0] * HALF + i * DEPTH, DEPTH)
        trio = (
            pltpu.make_async_copy(t_ref.at[:, cols], t.at[i], sems.at[i, 0]),
            pltpu.make_async_copy(source.at[rows, :], wt.at[i], sems.at[i, 1]),
            pltpu.make_async_copy(w_ref.at[pl.ds(start, DEPTH), :], wo.at[i], sems.at[i, 2]),
        )
        for copy in trio:
            copy.start()
        copies.append(trio)
    for i in range(count):
        for copy in copies[i]:
            copy.wait()
        theirs = jnp.dot(t[i], wt[i], preferred_element_type=jnp.float32)
        ours = jnp.dot(t[i], wo[i], preferred_element_type=jnp.float32)
        if i == 0:
            acc[...] = theirs
            ours_ref[...] = ours
        else:
            acc[...] += theirs
            ours_ref[...] += ours
    theirs_ref[...] = acc[...].astype(jnp.bfloat16)


def base_products(half, gathered, wa, wb, weight):
    count = HALF // DEPTH
    return pl.pallas_call(
        base_kernel,
        out_shape=[
            jax.ShapeDtypeStruct((ROWS, WIDTH), jnp.bfloat16),
            jax.ShapeDtypeStruct((ROWS, WIDTH), jnp.float32),
        ],
        in_specs=[SMEM, ANY, ANY, ANY, ANY],
        out_specs=[VMEM, VMEM],
        scratch_shapes=[
            pltpu.VMEM((count, ROWS, DEPTH), jnp.bfloat16),
            pltpu.VMEM((count, DEPTH, WIDTH), jnp.bfloat16),
            pltpu.VMEM((count, DEPTH, WIDTH), jnp.bfloat16),
            pltpu.VMEM((ROWS, WIDTH), jnp.float32),
            pltpu.SemaphoreType.DMA((count, 3)),
        ],
        compiler_params=vmem(56),
        cost_estimate=pl.CostEstimate(
            flops=4 * ROWS * HALF * WIDTH, bytes_accessed=10 << 20, transcendentals=0
        ),
    )(half, gathered, wa, wb, weight)


def last_kernel(
    ids_ref, stored_ref, seg_ref, dp_ref, low_ref, got_ref, ours_ref, recv_ref, out_ref, mats, sems
):
    copies = fetch(ids_ref, stored_ref, got_ref, mats, sems, 1)
    for copy in copies:
        copy.wait()
    for k in range(4):
        row, col = (k % 2) * SEG, (k // 2) * RANK
        low = low_ref[row : row + SEG, col : col + RANK]
        up = jnp.dot(low, mats[seg_ref[k] - 2 * dp_ref[0]], preferred_element_type=jnp.float32)
        rows = slice(k * SEG, (k + 1) * SEG)
        out_ref[rows, :] = (ours_ref[rows, :] + recv_ref[rows, :].astype(jnp.float32) + 2.0 * up).astype(jnp.bfloat16)


def last_product(ids, stored, seg, dp, low, got, ours, recv):
    return pl.pallas_call(
        last_kernel,
        out_shape=jax.ShapeDtypeStruct((ROWS, WIDTH), jnp.bfloat16),
        in_specs=[SMEM, SMEM, SMEM, SMEM, VMEM, ANY, VMEM, VMEM],
        out_specs=VMEM,
        scratch_shapes=[
            pltpu.VMEM((2, RANK, WIDTH), jnp.bfloat16),
            pltpu.SemaphoreType.DMA((2,)),
        ],
        compiler_params=vmem(8),
        cost_estimate=pl.CostEstimate(flops=1 << 24, bytes_accessed=2 << 20, transcendentals=0),
    )(ids, stored, seg, dp, low, got, ours, recv)


def body(tokens, weight, down, up, segment_request, request_ids, stored_row):
    xl = lax.axis_index("xl").astype(jnp.int32)
    dp = lax.axis_index(DP).astype(jnp.int32)[None]
    place = jnp.stack([lax.axis_index("xh"), lax.axis_index("zl")]).astype(jnp.int32)

    gathered = lax.all_gather(tokens, ("y", "c"), axis=1, tiled=True)

    spread = jnp.broadcast_to(request_ids[None, None, :], (PEERS, 1, 2))
    every_id = lax.all_to_all(spread, "zh", 0, 0, tiled=True)
    own, _ = lax.optimization_barrier((jnp.stack([down, up]), spread))
    pair = ("xh", "zl")
    far = [lax.ppermute(own, pair, [(i, i ^ flip) for i in range(4)]) for flip in (2, 1, 3)]

    sent = select(every_id, stored_row, place, own, *far)
    late_weight, _ = lax.optimization_barrier((weight, every_id))
    quarter = HALF // 2
    start = (1 - xl) * HALF
    wa = lax.ppermute(
        lax.dynamic_slice_in_dim(late_weight, start, quarter, 0), X, [(i, (i + 1) % 4) for i in range(4)]
    )
    wb = lax.ppermute(
        lax.dynamic_slice_in_dim(late_weight, start + quarter, quarter, 0),
        X,
        [(i, (i + 3) % 4) for i in range(4)],
    )

    got = lax.all_to_all(sent, "zh", 0, 0, tiled=True)

    partial = down_product(request_ids, stored_row, segment_request, dp, tokens, got)
    parts = lax.all_to_all(partial.reshape(32, 8, 128), TENSOR, 0, 0)
    low = lax.all_to_all(sum_parts(parts), TENSOR, 0, 0)

    weight, _ = lax.optimization_barrier((weight, partial))
    theirs, ours = base_products(xl[None], gathered, wa, wb, weight)
    recv = lax.ppermute(theirs, "xl", SWAP)
    return last_product(
        request_ids, stored_row, segment_request, dp, low.reshape(256, 128), got, ours, recv
    )


def solution(mesh):
    fine = Mesh(mesh.devices.reshape(2, 4, 2, 2, 8, 2), ("xh", "zh", "zl", "xl", "y", "c"))
    in_specs = (
        P(DP, TENSOR),
        P(None, TENSOR),
        P(DP, None, TENSOR),
        P(DP, None, TENSOR),
        P(DP),
        P(DP),
        P(),
    )
    return jax.shard_map(body, mesh=fine, in_specs=in_specs, out_specs=P(DP, TENSOR), check_vma=False)
```

```python
import jax
import jax.numpy as jnp
from jax import lax
from jax.experimental import pallas as pl
from jax.experimental.pallas import tpu as pltpu
from jax.sharding import Mesh, PartitionSpec as P

SWAP = [(0, 1), (1, 0)]
DP = ("xh", "zh", "zl")
X = ("xh", "xl")
TENSOR = ("xl", "y", "c")
ROWS = 512
SEG = 128
RANK = 64
WIDTH = 256
OWNED = 4
ZS = 8
PEERS = 4
SUM_TYPE = jnp.float32
HALF = 4096
DEPTH = 1024

ANY = pl.BlockSpec(memory_space=pl.ANY)
SMEM = pl.BlockSpec(memory_space=pltpu.SMEM)
VMEM = pl.BlockSpec(memory_space=pltpu.VMEM)


def vmem(mib):
    return pltpu.CompilerParams(vmem_limit_bytes=mib << 20)


def select_kernel(ids_ref, stored_ref, place_ref, own_ref, x_ref, z_ref, xz_ref, out_ref):
    held = (own_ref, x_ref, z_ref, xz_ref)
    for zh in range(PEERS):
        for r in range(2):
            row = stored_ref[ids_ref[zh, 0, r]]
            slot = row % OWNED
            owner = row // OWNED
            across_x = owner // ZS != place_ref[0]
            across_z = owner % 2 != place_ref[1]
            which = across_x.astype(jnp.int32) + 2 * across_z.astype(jnp.int32)
            for j in range(4):

                @pl.when(which == j)
                def _(zh=zh, r=r, slot=slot, j=j):
                    for part in range(2):
                        out_ref[zh, 2 * r + part] = held[j][part, slot]


def select(ids, stored, place, own, x, z, xz):
    return pl.pallas_call(
        select_kernel,
        out_shape=jax.ShapeDtypeStruct((PEERS, 4, RANK, WIDTH), own.dtype),
        in_specs=[SMEM, SMEM, SMEM, VMEM, VMEM, VMEM, VMEM],
        out_specs=VMEM,
        compiler_params=vmem(8),
        cost_estimate=pl.CostEstimate(flops=0, bytes_accessed=2 << 20, transcendentals=0),
    )(ids, stored, place, own, x, z, xz)


def fetch(ids_ref, stored_ref, got_ref, mats, sems, part):
    copies = []
    for r in range(2):
        source = stored_ref[ids_ref[r]] // OWNED % ZS // 2
        copy = pltpu.make_async_copy(got_ref.at[source, 2 * r + part], mats.at[r], sems.at[r])
        copy.start()
        copies.append(copy)
    return copies


def down_kernel(
    ids_ref, stored_ref, seg_ref, dp_ref, tokens_ref, got_ref, out_ref, ups_ref,
    mats, ups, sems, up_sems,
):
    copies = fetch(ids_ref, stored_ref, got_ref, mats, sems, 0)
    up_copies = fetch(ids_ref, stored_ref, got_ref, ups, up_sems, 1)
    for copy in copies:
        copy.wait()
    for k in range(4):
        part = lax.dot_general(
            tokens_ref[k * SEG : (k + 1) * SEG, :],
            mats[seg_ref[k] - 2 * dp_ref[0]],
            (((1,), (1,)), ((), ())),
            preferred_element_type=jnp.float32,
        )
        row, col = (k % 2) * SEG, (k // 2) * RANK
        out_ref[row : row + SEG, col : col + RANK] = part.astype(out_ref.dtype)
    for copy in up_copies:
        copy.wait()
    for k in range(4):
        ups_ref[k] = ups[seg_ref[k] - 2 * dp_ref[0]]


def down_product(ids, stored, seg, dp, tokens, got):
    mats = pltpu.VMEM((2, RANK, WIDTH), jnp.bfloat16)
    return pl.pallas_call(
        down_kernel,
        out_shape=[
            jax.ShapeDtypeStruct((256, 128), SUM_TYPE),
            jax.ShapeDtypeStruct((4, RANK, WIDTH), jnp.bfloat16),
        ],
        in_specs=[SMEM, SMEM, SMEM, SMEM, VMEM, ANY],
        out_specs=[VMEM, VMEM],
        scratch_shapes=[
            mats, mats, pltpu.SemaphoreType.DMA((2,)), pltpu.SemaphoreType.DMA((2,))
        ],
        compiler_params=vmem(4),
        cost_estimate=pl.CostEstimate(flops=1 << 24, bytes_accessed=1 << 20, transcendentals=0),
    )(ids, stored, seg, dp, tokens, got)


def sum_kernel(parts_ref, out_ref):
    total = jnp.sum(parts_ref[...].astype(jnp.float32), axis=0).astype(jnp.bfloat16)
    out_ref[...] = jnp.broadcast_to(total[None], out_ref.shape)


def sum_parts(parts):
    return pl.pallas_call(
        sum_kernel,
        out_shape=jax.ShapeDtypeStruct(parts.shape, jnp.bfloat16),
        in_specs=[VMEM],
        out_specs=VMEM,
        compiler_params=vmem(4),
        cost_estimate=pl.CostEstimate(flops=0, bytes_accessed=128 << 20, transcendentals=0),
    )(parts)


def base_kernel(half_ref, t_ref, wa_ref, wb_ref, w_ref, theirs_ref, ours_ref, t, wt, wo, acc, sems):
    count = HALF // DEPTH
    per_quarter = count // 2
    copies = []
    for i in range(count):
        cols = slice(i * DEPTH, (i + 1) * DEPTH)
        source = wa_ref if i < per_quarter else wb_ref
        rows = pl.ds((i % per_quarter) * DEPTH, DEPTH)
        start = pl.multiple_of(half_ref[0] * HALF + i * DEPTH, DEPTH)
        trio = (
            pltpu.make_async_copy(t_ref.at[:, cols], t.at[i], sems.at[i, 0]),
            pltpu.make_async_copy(source.at[rows, :], wt.at[i], sems.at[i, 1]),
            pltpu.make_async_copy(w_ref.at[pl.ds(start, DEPTH), :], wo.at[i], sems.at[i, 2]),
        )
        for copy in trio:
            copy.start()
        copies.append(trio)
    for i in range(count):
        for copy in copies[i]:
            copy.wait()
        theirs = jnp.dot(t[i], wt[i], preferred_element_type=jnp.float32)
        ours = jnp.dot(t[i], wo[i], preferred_element_type=jnp.float32)
        if i == 0:
            acc[...] = theirs
            ours_ref[...] = ours
        else:
            acc[...] += theirs
            ours_ref[...] += ours
    theirs_ref[...] = acc[...].astype(jnp.bfloat16)


def base_products(half, gathered, wa, wb, weight):
    count = HALF // DEPTH
    return pl.pallas_call(
        base_kernel,
        out_shape=[
            jax.ShapeDtypeStruct((ROWS, WIDTH), jnp.bfloat16),
            jax.ShapeDtypeStruct((ROWS, WIDTH), jnp.float32),
        ],
        in_specs=[SMEM, ANY, ANY, ANY, ANY],
        out_specs=[VMEM, VMEM],
        scratch_shapes=[
            pltpu.VMEM((count, ROWS, DEPTH), jnp.bfloat16),
            pltpu.VMEM((count, DEPTH, WIDTH), jnp.bfloat16),
            pltpu.VMEM((count, DEPTH, WIDTH), jnp.bfloat16),
            pltpu.VMEM((ROWS, WIDTH), jnp.float32),
            pltpu.SemaphoreType.DMA((count, 3)),
        ],
        compiler_params=vmem(56),
        cost_estimate=pl.CostEstimate(
            flops=4 * ROWS * HALF * WIDTH, bytes_accessed=10 << 20, transcendentals=0
        ),
    )(half, gathered, wa, wb, weight)


def add_kernel(ours_ref, recv_ref, out_ref):
    out_ref[...] = ours_ref[...] + recv_ref[...].astype(jnp.float32)


def add(ours, recv):
    return pl.pallas_call(
        add_kernel,
        out_shape=jax.ShapeDtypeStruct((ROWS, WIDTH), jnp.float32),
        in_specs=[VMEM, VMEM],
        out_specs=VMEM,
        compiler_params=vmem(8),
        cost_estimate=pl.CostEstimate(flops=1 << 17, bytes_accessed=2 << 20, transcendentals=0),
    )(ours, recv)


def last_kernel(low_ref, ups_ref, base_ref, out_ref):
    for k in range(4):
        row, col = (k % 2) * SEG, (k // 2) * RANK
        low = low_ref[row : row + SEG, col : col + RANK]
        up = jnp.dot(low, ups_ref[k], preferred_element_type=jnp.float32)
        rows = slice(k * SEG, (k + 1) * SEG)
        out_ref[rows, :] = (base_ref[rows, :] + 2.0 * up).astype(jnp.bfloat16)


def last_product(low, ups, base):
    return pl.pallas_call(
        last_kernel,
        out_shape=jax.ShapeDtypeStruct((ROWS, WIDTH), jnp.bfloat16),
        in_specs=[VMEM, VMEM, VMEM],
        out_specs=VMEM,
        compiler_params=vmem(8),
        cost_estimate=pl.CostEstimate(flops=1 << 24, bytes_accessed=2 << 20, transcendentals=0),
    )(low, ups, base)


def body(tokens, weight, down, up, segment_request, request_ids, stored_row):
    xl = lax.axis_index("xl").astype(jnp.int32)
    dp = lax.axis_index(DP).astype(jnp.int32)[None]
    place = jnp.stack([lax.axis_index("xh"), lax.axis_index("zl")]).astype(jnp.int32)

    gathered = lax.all_gather(tokens, ("y", "c"), axis=1, tiled=True)

    spread = jnp.broadcast_to(request_ids[None, None, :], (PEERS, 1, 2))
    every_id = lax.all_to_all(spread, "zh", 0, 0, tiled=True)
    own, _ = lax.optimization_barrier((jnp.stack([down, up]), spread))
    pair = ("xh", "zl")
    far = [lax.ppermute(own, pair, [(i, i ^ flip) for i in range(4)]) for flip in (2, 1, 3)]

    sent = select(every_id, stored_row, place, own, *far)
    late_weight, _ = lax.optimization_barrier((weight, every_id))
    quarter = HALF // 2
    start = (1 - xl) * HALF
    wa = lax.ppermute(
        lax.dynamic_slice_in_dim(late_weight, start, quarter, 0), X, [(i, (i + 1) % 4) for i in range(4)]
    )
    wb = lax.ppermute(
        lax.dynamic_slice_in_dim(late_weight, start + quarter, quarter, 0),
        X,
        [(i, (i + 3) % 4) for i in range(4)],
    )

    got = lax.all_to_all(sent, "zh", 0, 0, tiled=True)

    partial, ups = down_product(request_ids, stored_row, segment_request, dp, tokens, got)
    parts = lax.all_to_all(partial.reshape(32, 8, 128), TENSOR, 0, 0)
    low = lax.all_to_all(sum_parts(parts), TENSOR, 0, 0)

    weight, _ = lax.optimization_barrier((weight, partial))
    theirs, ours = base_products(xl[None], gathered, wa, wb, weight)
    recv = lax.ppermute(theirs, "xl", SWAP)
    return last_product(low.reshape(256, 128), ups, add(ours, recv))


def solution(mesh):
    fine = Mesh(mesh.devices.reshape(2, 4, 2, 2, 8, 2), ("xh", "zh", "zl", "xl", "y", "c"))
    in_specs = (
        P(DP, TENSOR),
        P(None, TENSOR),
        P(DP, None, TENSOR),
        P(DP, None, TENSOR),
        P(DP),
        P(DP),
        P(),
    )
    return jax.shard_map(body, mesh=fine, in_specs=in_specs, out_specs=P(DP, TENSOR), check_vma=False)
```

```python
import jax
import jax.numpy as jnp
from jax import lax
from jax.experimental import pallas as pl
from jax.experimental.pallas import tpu as pltpu
from jax.sharding import Mesh, PartitionSpec as P

SWAP = [(0, 1), (1, 0)]
DP = ("xh", "zh", "zl")
X = ("xh", "xl")
TENSOR = ("xl", "y", "c")
ROWS = 512
SEG = 128
RANK = 64
WIDTH = 256
OWNED = 4
ZS = 8
PEERS = 4
SUM_TYPE = jnp.float32
HALF = 4096
DEPTH = 1024

ANY = pl.BlockSpec(memory_space=pl.ANY)
SMEM = pl.BlockSpec(memory_space=pltpu.SMEM)
VMEM = pl.BlockSpec(memory_space=pltpu.VMEM)


def vmem(mib):
    return pltpu.CompilerParams(vmem_limit_bytes=mib << 20)


def select_kernel(ids_ref, stored_ref, place_ref, own_ref, x_ref, z_ref, xz_ref, out_ref):
    held = (own_ref, x_ref, z_ref, xz_ref)
    for zh in range(PEERS):
        for r in range(2):
            row = stored_ref[ids_ref[zh, 0, r]]
            slot = row % OWNED
            owner = row // OWNED
            across_x = owner // ZS != place_ref[0]
            across_z = owner % 2 != place_ref[1]
            which = across_x.astype(jnp.int32) + 2 * across_z.astype(jnp.int32)
            for j in range(4):

                @pl.when(which == j)
                def _(zh=zh, r=r, slot=slot, j=j):
                    for part in range(2):
                        out_ref[zh, 2 * r + part] = held[j][part, slot]


def select(ids, stored, place, own, x, z, xz):
    return pl.pallas_call(
        select_kernel,
        out_shape=jax.ShapeDtypeStruct((PEERS, 4, RANK, WIDTH), own.dtype),
        in_specs=[SMEM, SMEM, SMEM, VMEM, VMEM, VMEM, VMEM],
        out_specs=VMEM,
        compiler_params=vmem(8),
        cost_estimate=pl.CostEstimate(flops=0, bytes_accessed=2 << 20, transcendentals=0),
    )(ids, stored, place, own, x, z, xz)


def fetch(ids_ref, stored_ref, got_ref, mats, sems, part):
    copies = []
    for r in range(2):
        source = stored_ref[ids_ref[r]] // OWNED % ZS // 2
        copy = pltpu.make_async_copy(got_ref.at[source, 2 * r + part], mats.at[r], sems.at[r])
        copy.start()
        copies.append(copy)
    return copies


def down_kernel(
    ids_ref, stored_ref, seg_ref, dp_ref, tokens_ref, got_ref, out_ref, ups_ref,
    mats, ups, sems, up_sems,
):
    copies = fetch(ids_ref, stored_ref, got_ref, mats, sems, 0)
    up_copies = fetch(ids_ref, stored_ref, got_ref, ups, up_sems, 1)
    for copy in copies:
        copy.wait()
    for k in range(4):
        part = lax.dot_general(
            tokens_ref[k * SEG : (k + 1) * SEG, :],
            mats[seg_ref[k] - 2 * dp_ref[0]],
            (((1,), (1,)), ((), ())),
            preferred_element_type=jnp.float32,
        )
        row, col = (k % 2) * SEG, (k // 2) * RANK
        out_ref[row : row + SEG, col : col + RANK] = part.astype(out_ref.dtype)
    for copy in up_copies:
        copy.wait()
    for k in range(4):
        ups_ref[k] = ups[seg_ref[k] - 2 * dp_ref[0]]


def down_product(ids, stored, seg, dp, tokens, got):
    mats = pltpu.VMEM((2, RANK, WIDTH), jnp.bfloat16)
    return pl.pallas_call(
        down_kernel,
        out_shape=[
            jax.ShapeDtypeStruct((256, 128), SUM_TYPE),
            jax.ShapeDtypeStruct((4, RANK, WIDTH), jnp.bfloat16),
        ],
        in_specs=[SMEM, SMEM, SMEM, SMEM, VMEM, ANY],
        out_specs=[VMEM, VMEM],
        scratch_shapes=[
            mats, mats, pltpu.SemaphoreType.DMA((2,)), pltpu.SemaphoreType.DMA((2,))
        ],
        compiler_params=vmem(4),
        cost_estimate=pl.CostEstimate(flops=1 << 24, bytes_accessed=1 << 20, transcendentals=0),
    )(ids, stored, seg, dp, tokens, got)


def sum_kernel(parts_ref, out_ref):
    total = jnp.sum(parts_ref[...].astype(jnp.float32), axis=0).astype(jnp.bfloat16)
    out_ref[...] = jnp.broadcast_to(total[None], out_ref.shape)


def sum_parts(parts):
    return pl.pallas_call(
        sum_kernel,
        out_shape=jax.ShapeDtypeStruct(parts.shape, jnp.bfloat16),
        in_specs=[VMEM],
        out_specs=VMEM,
        compiler_params=vmem(4),
        cost_estimate=pl.CostEstimate(flops=0, bytes_accessed=128 << 20, transcendentals=0),
    )(parts)


def base_kernel(half_ref, t_ref, wa_ref, wb_ref, w_ref, theirs_ref, ours_ref, t, wo, acc, sems):
    count = HALF // DEPTH
    per_quarter = count // 2
    copies = []
    for i in range(count):
        cols = slice(i * DEPTH, (i + 1) * DEPTH)
        start = pl.multiple_of(half_ref[0] * HALF + i * DEPTH, DEPTH)
        pair = (
            pltpu.make_async_copy(t_ref.at[:, cols], t.at[i], sems.at[i, 0]),
            pltpu.make_async_copy(w_ref.at[pl.ds(start, DEPTH), :], wo.at[i], sems.at[i, 1]),
        )
        for copy in pair:
            copy.start()
        copies.append(pair)
    for i in range(count):
        for copy in copies[i]:
            copy.wait()
        source = wa_ref if i < per_quarter else wb_ref
        rows = slice((i % per_quarter) * DEPTH, (i % per_quarter + 1) * DEPTH)
        theirs = jnp.dot(t[i], source[rows, :], preferred_element_type=jnp.float32)
        ours = jnp.dot(t[i], wo[i], preferred_element_type=jnp.float32)
        if i == 0:
            acc[...] = theirs
            ours_ref[...] = ours
        else:
            acc[...] += theirs
            ours_ref[...] += ours
    theirs_ref[...] = acc[...].astype(jnp.bfloat16)


def base_products(half, gathered, wa, wb, weight):
    count = HALF // DEPTH
    return pl.pallas_call(
        base_kernel,
        out_shape=[
            jax.ShapeDtypeStruct((ROWS, WIDTH), jnp.bfloat16),
            jax.ShapeDtypeStruct((ROWS, WIDTH), jnp.float32),
        ],
        in_specs=[SMEM, ANY, VMEM, VMEM, ANY],
        out_specs=[VMEM, VMEM],
        scratch_shapes=[
            pltpu.VMEM((count, ROWS, DEPTH), jnp.bfloat16),
            pltpu.VMEM((count, DEPTH, WIDTH), jnp.bfloat16),
            pltpu.VMEM((ROWS, WIDTH), jnp.float32),
            pltpu.SemaphoreType.DMA((count, 2)),
        ],
        compiler_params=vmem(51),
        cost_estimate=pl.CostEstimate(
            flops=4 * ROWS * HALF * WIDTH, bytes_accessed=10 << 20, transcendentals=0
        ),
    )(half, gathered, wa, wb, weight)


def add_kernel(ours_ref, recv_ref, out_ref):
    out_ref[...] = ours_ref[...] + recv_ref[...].astype(jnp.float32)


def add(ours, recv):
    return pl.pallas_call(
        add_kernel,
        out_shape=jax.ShapeDtypeStruct((ROWS, WIDTH), jnp.float32),
        in_specs=[VMEM, VMEM],
        out_specs=VMEM,
        compiler_params=vmem(8),
        cost_estimate=pl.CostEstimate(flops=1 << 17, bytes_accessed=2 << 20, transcendentals=0),
    )(ours, recv)


def last_kernel(low_ref, ups_ref, base_ref, out_ref):
    for k in range(4):
        row, col = (k % 2) * SEG, (k // 2) * RANK
        low = low_ref[row : row + SEG, col : col + RANK]
        up = jnp.dot(low, ups_ref[k], preferred_element_type=jnp.float32)
        rows = slice(k * SEG, (k + 1) * SEG)
        out_ref[rows, :] = (base_ref[rows, :] + 2.0 * up).astype(jnp.bfloat16)


def last_product(low, ups, base):
    return pl.pallas_call(
        last_kernel,
        out_shape=jax.ShapeDtypeStruct((ROWS, WIDTH), jnp.bfloat16),
        in_specs=[VMEM, VMEM, VMEM],
        out_specs=VMEM,
        compiler_params=vmem(8),
        cost_estimate=pl.CostEstimate(flops=1 << 24, bytes_accessed=2 << 20, transcendentals=0),
    )(low, ups, base)


def body(tokens, weight, down, up, segment_request, request_ids, stored_row):
    xl = lax.axis_index("xl").astype(jnp.int32)
    dp = lax.axis_index(DP).astype(jnp.int32)[None]
    place = jnp.stack([lax.axis_index("xh"), lax.axis_index("zl")]).astype(jnp.int32)

    spread = jnp.broadcast_to(request_ids[None, None, :], (PEERS, 1, 2))
    late_tokens, _ = lax.optimization_barrier((tokens, spread))
    gathered = lax.all_gather(late_tokens, ("y", "c"), axis=1, tiled=True)
    every_id = lax.all_to_all(spread, "zh", 0, 0, tiled=True)
    own, _ = lax.optimization_barrier((jnp.stack([down, up]), spread))
    pair = ("xh", "zl")
    far = [lax.ppermute(own, pair, [(i, i ^ flip) for i in range(4)]) for flip in (2, 1, 3)]

    sent = select(every_id, stored_row, place, own, *far)
    late_weight, _ = lax.optimization_barrier((weight, every_id))
    quarter = HALF // 2
    start = (1 - xl) * HALF
    wa = lax.ppermute(
        lax.dynamic_slice_in_dim(late_weight, start, quarter, 0), X, [(i, (i + 1) % 4) for i in range(4)]
    )
    wb = lax.ppermute(
        lax.dynamic_slice_in_dim(late_weight, start + quarter, quarter, 0),
        X,
        [(i, (i + 3) % 4) for i in range(4)],
    )

    got = lax.all_to_all(sent, "zh", 0, 0, tiled=True)

    partial, ups = down_product(request_ids, stored_row, segment_request, dp, tokens, got)
    parts = lax.all_to_all(partial.reshape(32, 8, 128), TENSOR, 0, 0)
    low = lax.all_to_all(sum_parts(parts), TENSOR, 0, 0)

    weight, _ = lax.optimization_barrier((weight, partial))
    theirs, ours = base_products(xl[None], gathered, wa, wb, weight)
    recv = lax.ppermute(theirs, "xl", SWAP)
    return last_product(low.reshape(256, 128), ups, add(ours, recv))


def solution(mesh):
    fine = Mesh(mesh.devices.reshape(2, 4, 2, 2, 8, 2), ("xh", "zh", "zl", "xl", "y", "c"))
    in_specs = (
        P(DP, TENSOR),
        P(None, TENSOR),
        P(DP, None, TENSOR),
        P(DP, None, TENSOR),
        P(DP),
        P(DP),
        P(),
    )
    return jax.shard_map(body, mesh=fine, in_specs=in_specs, out_specs=P(DP, TENSOR), check_vma=False)
```

```python
import jax
import jax.numpy as jnp
from jax import lax
from jax.experimental import pallas as pl
from jax.experimental.pallas import tpu as pltpu
from jax.sharding import Mesh, PartitionSpec as P

SWAP = [(0, 1), (1, 0)]
DP = ("xh", "zh", "zl")
X = ("xh", "xl")
TENSOR = ("xl", "y", "c")
ROWS = 512
SEG = 128
RANK = 64
WIDTH = 256
OWNED = 4
ZS = 8
PEERS = 4
HALF = 4096
DEPTH = 1024

ANY = pl.BlockSpec(memory_space=pl.ANY)
SMEM = pl.BlockSpec(memory_space=pltpu.SMEM)
VMEM = pl.BlockSpec(memory_space=pltpu.VMEM)


def vmem(mib):
    return pltpu.CompilerParams(vmem_limit_bytes=mib << 20)


def select_kernel(ids_ref, stored_ref, place_ref, own_ref, x_ref, z_ref, xz_ref, out_ref):
    held = (own_ref, x_ref, z_ref, xz_ref)
    for zh in range(PEERS):
        for r in range(2):
            row = stored_ref[ids_ref[zh, 0, r]]
            slot = row % OWNED
            owner = row // OWNED
            across_x = owner // ZS != place_ref[0]
            across_z = owner % 2 != place_ref[1]
            which = across_x.astype(jnp.int32) + 2 * across_z.astype(jnp.int32)
            for j in range(4):

                @pl.when(which == j)
                def _(zh=zh, r=r, slot=slot, j=j):
                    for part in range(2):
                        out_ref[zh, 2 * r + part] = held[j][part, slot]


def select(ids, stored, place, own, x, z, xz):
    return pl.pallas_call(
        select_kernel,
        out_shape=jax.ShapeDtypeStruct((PEERS, 4, RANK, WIDTH), own.dtype),
        in_specs=[SMEM, SMEM, SMEM, VMEM, VMEM, VMEM, VMEM],
        out_specs=VMEM,
        compiler_params=vmem(8),
        cost_estimate=pl.CostEstimate(flops=0, bytes_accessed=2 << 20, transcendentals=0),
    )(ids, stored, place, own, x, z, xz)


def fetch(ids_ref, stored_ref, got_ref, mats, sems, part):
    copies = []
    for r in range(2):
        source = stored_ref[ids_ref[r]] // OWNED % ZS // 2
        copy = pltpu.make_async_copy(got_ref.at[source, 2 * r + part], mats.at[r], sems.at[r])
        copy.start()
        copies.append(copy)
    return copies


def down_kernel(ids_ref, stored_ref, seg_ref, dp_ref, tokens_ref, got_ref, out_ref, mats, sems):
    for copy in fetch(ids_ref, stored_ref, got_ref, mats, sems, 0):
        copy.wait()
    for k in range(4):
        part = lax.dot_general(
            tokens_ref[k * SEG : (k + 1) * SEG, :],
            mats[seg_ref[k] - 2 * dp_ref[0]],
            (((1,), (1,)), ((), ())),
            preferred_element_type=jnp.float32,
        )
        row, col = (k % 2) * SEG, (k // 2) * RANK
        out_ref[row : row + SEG, col : col + RANK] = part


def down_product(ids, stored, seg, dp, tokens, got):
    return pl.pallas_call(
        down_kernel,
        out_shape=jax.ShapeDtypeStruct((256, 128), jnp.float32),
        in_specs=[SMEM, SMEM, SMEM, SMEM, VMEM, ANY],
        out_specs=VMEM,
        scratch_shapes=[
            pltpu.VMEM((2, RANK, WIDTH), jnp.bfloat16),
            pltpu.SemaphoreType.DMA((2,)),
        ],
        compiler_params=vmem(4),
        cost_estimate=pl.CostEstimate(flops=1 << 24, bytes_accessed=1 << 20, transcendentals=0),
    )(ids, stored, seg, dp, tokens, got)


def pick_kernel(ids_ref, stored_ref, seg_ref, dp_ref, got_ref, out_ref, mats, sems):
    for copy in fetch(ids_ref, stored_ref, got_ref, mats, sems, 1):
        copy.wait()
    for k in range(4):
        out_ref[k] = mats[seg_ref[k] - 2 * dp_ref[0]]


def pick(ids, stored, seg, dp, got):
    return pl.pallas_call(
        pick_kernel,
        out_shape=jax.ShapeDtypeStruct((4, RANK, WIDTH), jnp.bfloat16),
        in_specs=[SMEM, SMEM, SMEM, SMEM, ANY],
        out_specs=VMEM,
        scratch_shapes=[
            pltpu.VMEM((2, RANK, WIDTH), jnp.bfloat16),
            pltpu.SemaphoreType.DMA((2,)),
        ],
        compiler_params=vmem(4),
        cost_estimate=pl.CostEstimate(flops=0, bytes_accessed=1 << 18, transcendentals=0),
    )(ids, stored, seg, dp, got)


def sum_kernel(parts_ref, out_ref):
    total = jnp.sum(parts_ref[...].astype(jnp.float32), axis=0).astype(jnp.bfloat16)
    out_ref[...] = jnp.broadcast_to(total[None], out_ref.shape)


def sum_parts(parts):
    return pl.pallas_call(
        sum_kernel,
        out_shape=jax.ShapeDtypeStruct(parts.shape, jnp.bfloat16),
        in_specs=[VMEM],
        out_specs=VMEM,
        compiler_params=vmem(4),
        cost_estimate=pl.CostEstimate(flops=0, bytes_accessed=128 << 20, transcendentals=0),
    )(parts)


def base_kernel(half_ref, t_ref, wa_ref, wb_ref, w_ref, theirs_ref, ours_ref, t, wo, acc, sems):
    count = HALF // DEPTH
    per_quarter = count // 2
    copies = []
    for i in range(count):
        cols = slice(i * DEPTH, (i + 1) * DEPTH)
        start = pl.multiple_of(half_ref[0] * HALF + i * DEPTH, DEPTH)
        pair = (
            pltpu.make_async_copy(t_ref.at[:, cols], t.at[i], sems.at[i, 0]),
            pltpu.make_async_copy(w_ref.at[pl.ds(start, DEPTH), :], wo.at[i], sems.at[i, 1]),
        )
        for copy in pair:
            copy.start()
        copies.append(pair)
    for i in range(count):
        for copy in copies[i]:
            copy.wait()
        source = wa_ref if i < per_quarter else wb_ref
        rows = slice((i % per_quarter) * DEPTH, (i % per_quarter + 1) * DEPTH)
        theirs = jnp.dot(t[i], source[rows, :], preferred_element_type=jnp.float32)
        ours = jnp.dot(t[i], wo[i], preferred_element_type=jnp.float32)
        if i == 0:
            acc[...] = theirs
            ours_ref[...] = ours
        else:
            acc[...] += theirs
            ours_ref[...] += ours
    theirs_ref[...] = acc[...].astype(jnp.bfloat16)


def base_products(half, gathered, wa, wb, weight):
    count = HALF // DEPTH
    return pl.pallas_call(
        base_kernel,
        out_shape=[
            jax.ShapeDtypeStruct((ROWS, WIDTH), jnp.bfloat16),
            jax.ShapeDtypeStruct((ROWS, WIDTH), jnp.float32),
        ],
        in_specs=[SMEM, ANY, VMEM, VMEM, ANY],
        out_specs=[VMEM, VMEM],
        scratch_shapes=[
            pltpu.VMEM((count, ROWS, DEPTH), jnp.bfloat16),
            pltpu.VMEM((count, DEPTH, WIDTH), jnp.bfloat16),
            pltpu.VMEM((ROWS, WIDTH), jnp.float32),
            pltpu.SemaphoreType.DMA((count, 2)),
        ],
        compiler_params=vmem(51),
        cost_estimate=pl.CostEstimate(
            flops=4 * ROWS * HALF * WIDTH, bytes_accessed=10 << 20, transcendentals=0
        ),
    )(half, gathered, wa, wb, weight)


def add_kernel(ours_ref, recv_ref, out_ref):
    out_ref[...] = ours_ref[...] + recv_ref[...].astype(jnp.float32)


def add(ours, recv):
    return pl.pallas_call(
        add_kernel,
        out_shape=jax.ShapeDtypeStruct((ROWS, WIDTH), jnp.float32),
        in_specs=[VMEM, VMEM],
        out_specs=VMEM,
        compiler_params=vmem(8),
        cost_estimate=pl.CostEstimate(flops=1 << 17, bytes_accessed=2 << 20, transcendentals=0),
    )(ours, recv)


def last_kernel(low_ref, ups_ref, base_ref, out_ref):
    for k in range(4):
        row, col = (k % 2) * SEG, (k // 2) * RANK
        low = low_ref[row : row + SEG, col : col + RANK]
        up = jnp.dot(low, ups_ref[k], preferred_element_type=jnp.float32)
        rows = slice(k * SEG, (k + 1) * SEG)
        out_ref[rows, :] = (base_ref[rows, :] + 2.0 * up).astype(jnp.bfloat16)


def last_product(low, ups, base):
    return pl.pallas_call(
        last_kernel,
        out_shape=jax.ShapeDtypeStruct((ROWS, WIDTH), jnp.bfloat16),
        in_specs=[VMEM, VMEM, VMEM],
        out_specs=VMEM,
        compiler_params=vmem(8),
        cost_estimate=pl.CostEstimate(flops=1 << 24, bytes_accessed=2 << 20, transcendentals=0),
    )(low, ups, base)


def body(tokens, weight, down, up, segment_request, request_ids, stored_row):
    xl = lax.axis_index("xl").astype(jnp.int32)
    dp = lax.axis_index(DP).astype(jnp.int32)[None]
    place = jnp.stack([lax.axis_index("xh"), lax.axis_index("zl")]).astype(jnp.int32)

    spread = jnp.broadcast_to(request_ids[None, None, :], (PEERS, 1, 2))
    late_tokens, _ = lax.optimization_barrier((tokens, spread))
    gathered = lax.all_gather(late_tokens, ("y", "c"), axis=1, tiled=True)
    every_id = lax.all_to_all(spread, "zh", 0, 0, tiled=True)
    own, _ = lax.optimization_barrier((jnp.stack([down, up]), spread))
    pair = ("xh", "zl")
    far = [lax.ppermute(own, pair, [(i, i ^ flip) for i in range(4)]) for flip in (2, 1, 3)]

    sent = select(every_id, stored_row, place, own, *far)
    late_weight, _ = lax.optimization_barrier((weight, every_id))
    quarter = HALF // 2
    start = (1 - xl) * HALF
    wa = lax.ppermute(
        lax.dynamic_slice_in_dim(late_weight, start, quarter, 0), X, [(i, (i + 1) % 4) for i in range(4)]
    )
    wb = lax.ppermute(
        lax.dynamic_slice_in_dim(late_weight, start + quarter, quarter, 0),
        X,
        [(i, (i + 3) % 4) for i in range(4)],
    )

    got = lax.all_to_all(sent, "zh", 0, 0, tiled=True)

    partial = down_product(request_ids, stored_row, segment_request, dp, tokens, got)
    parts = lax.all_to_all(partial.reshape(32, 8, 128), TENSOR, 0, 0)
    low = lax.all_to_all(sum_parts(parts), TENSOR, 0, 0)

    weight, _ = lax.optimization_barrier((weight, partial))
    theirs, ours = base_products(xl[None], gathered, wa, wb, weight)
    recv = lax.ppermute(theirs, "xl", SWAP)
    ups = pick(request_ids, stored_row, segment_request, dp, got)
    return last_product(low.reshape(256, 128), ups, add(ours, recv))


def solution(mesh):
    fine = Mesh(mesh.devices.reshape(2, 4, 2, 2, 8, 2), ("xh", "zh", "zl", "xl", "y", "c"))
    in_specs = (
        P(DP, TENSOR),
        P(None, TENSOR),
        P(DP, None, TENSOR),
        P(DP, None, TENSOR),
        P(DP),
        P(DP),
        P(),
    )
    return jax.shard_map(body, mesh=fine, in_specs=in_specs, out_specs=P(DP, TENSOR), check_vma=False)
```

```python
import jax
import jax.numpy as jnp
from jax import lax
from jax.experimental import pallas as pl
from jax.experimental.pallas import tpu as pltpu
from jax.sharding import Mesh, PartitionSpec as P

SWAP = [(0, 1), (1, 0)]
DP = ("xh", "zh", "zl")
X = ("xh", "xl")
TENSOR = ("xl", "y", "c")
ROWS = 512
SEG = 128
RANK = 64
WIDTH = 256
OWNED = 4
ZS = 8
PEERS = 4
HALF = 4096
DEPTH = 512

ANY = pl.BlockSpec(memory_space=pl.ANY)
SMEM = pl.BlockSpec(memory_space=pltpu.SMEM)
VMEM = pl.BlockSpec(memory_space=pltpu.VMEM)


def vmem(mib):
    return pltpu.CompilerParams(vmem_limit_bytes=mib << 20)


def select_kernel(ids_ref, stored_ref, place_ref, own_ref, x_ref, z_ref, xz_ref, out_ref):
    held = (own_ref, x_ref, z_ref, xz_ref)
    for zh in range(PEERS):
        for r in range(2):
            row = stored_ref[ids_ref[zh, 0, r]]
            slot = row % OWNED
            owner = row // OWNED
            across_x = owner // ZS != place_ref[0]
            across_z = owner % 2 != place_ref[1]
            which = across_x.astype(jnp.int32) + 2 * across_z.astype(jnp.int32)
            for j in range(4):

                @pl.when(which == j)
                def _(zh=zh, r=r, slot=slot, j=j):
                    for part in range(2):
                        out_ref[zh, 2 * r + part] = held[j][part, slot]


def select(ids, stored, place, own, x, z, xz):
    return pl.pallas_call(
        select_kernel,
        out_shape=jax.ShapeDtypeStruct((PEERS, 4, RANK, WIDTH), own.dtype),
        in_specs=[SMEM, SMEM, SMEM, VMEM, VMEM, VMEM, VMEM],
        out_specs=VMEM,
        compiler_params=vmem(8),
        cost_estimate=pl.CostEstimate(flops=0, bytes_accessed=2 << 20, transcendentals=0),
    )(ids, stored, place, own, x, z, xz)


def fetch(ids_ref, stored_ref, got_ref, mats, sems, part):
    copies = []
    for r in range(2):
        source = stored_ref[ids_ref[r]] // OWNED % ZS // 2
        copy = pltpu.make_async_copy(got_ref.at[source, 2 * r + part], mats.at[r], sems.at[r])
        copy.start()
        copies.append(copy)
    return copies


def down_kernel(ids_ref, stored_ref, seg_ref, dp_ref, tokens_ref, got_ref, out_ref, mats, sems):
    for copy in fetch(ids_ref, stored_ref, got_ref, mats, sems, 0):
        copy.wait()
    for k in range(4):
        part = lax.dot_general(
            tokens_ref[k * SEG : (k + 1) * SEG, :],
            mats[seg_ref[k] - 2 * dp_ref[0]],
            (((1,), (1,)), ((), ())),
            preferred_element_type=jnp.float32,
        )
        row, col = (k % 2) * SEG, (k // 2) * RANK
        out_ref[row : row + SEG, col : col + RANK] = part


def down_product(ids, stored, seg, dp, tokens, got):
    return pl.pallas_call(
        down_kernel,
        out_shape=jax.ShapeDtypeStruct((256, 128), jnp.float32),
        in_specs=[SMEM, SMEM, SMEM, SMEM, VMEM, ANY],
        out_specs=VMEM,
        scratch_shapes=[
            pltpu.VMEM((2, RANK, WIDTH), jnp.bfloat16),
            pltpu.SemaphoreType.DMA((2,)),
        ],
        compiler_params=vmem(4),
        cost_estimate=pl.CostEstimate(flops=1 << 24, bytes_accessed=1 << 20, transcendentals=0),
    )(ids, stored, seg, dp, tokens, got)


def pick_kernel(ids_ref, stored_ref, seg_ref, dp_ref, got_ref, out_ref, mats, sems):
    for copy in fetch(ids_ref, stored_ref, got_ref, mats, sems, 1):
        copy.wait()
    for k in range(4):
        out_ref[k] = mats[seg_ref[k] - 2 * dp_ref[0]]


def pick(ids, stored, seg, dp, got):
    return pl.pallas_call(
        pick_kernel,
        out_shape=jax.ShapeDtypeStruct((4, RANK, WIDTH), jnp.bfloat16),
        in_specs=[SMEM, SMEM, SMEM, SMEM, ANY],
        out_specs=VMEM,
        scratch_shapes=[
            pltpu.VMEM((2, RANK, WIDTH), jnp.bfloat16),
            pltpu.SemaphoreType.DMA((2,)),
        ],
        compiler_params=vmem(4),
        cost_estimate=pl.CostEstimate(flops=0, bytes_accessed=1 << 18, transcendentals=0),
    )(ids, stored, seg, dp, got)


def sum_kernel(parts_ref, out_ref):
    total = jnp.sum(parts_ref[...].astype(jnp.float32), axis=0).astype(jnp.bfloat16)
    out_ref[...] = jnp.broadcast_to(total[None], out_ref.shape)


def sum_parts(parts):
    return pl.pallas_call(
        sum_kernel,
        out_shape=jax.ShapeDtypeStruct(parts.shape, jnp.bfloat16),
        in_specs=[VMEM],
        out_specs=VMEM,
        compiler_params=vmem(4),
        cost_estimate=pl.CostEstimate(flops=0, bytes_accessed=128 << 20, transcendentals=0),
    )(parts)


def base_kernel(half_ref, t_ref, wa_ref, wb_ref, w_ref, theirs_ref, ours_ref, t, wt, wo, acc, sems):
    count = HALF // DEPTH
    per_quarter = count // 2
    copies = []
    for i in range(count):
        cols = slice(i * DEPTH, (i + 1) * DEPTH)
        source = wa_ref if i < per_quarter else wb_ref
        rows = pl.ds((i % per_quarter) * DEPTH, DEPTH)
        start = pl.multiple_of(half_ref[0] * HALF + i * DEPTH, DEPTH)
        trio = (
            pltpu.make_async_copy(t_ref.at[:, cols], t.at[i], sems.at[i, 0]),
            pltpu.make_async_copy(source.at[rows, :], wt.at[i], sems.at[i, 1]),
            pltpu.make_async_copy(w_ref.at[pl.ds(start, DEPTH), :], wo.at[i], sems.at[i, 2]),
        )
        for copy in trio:
            copy.start()
        copies.append(trio)
    for i in range(count):
        for copy in copies[i]:
            copy.wait()
        theirs = jnp.dot(t[i], wt[i], preferred_element_type=jnp.float32)
        ours = jnp.dot(t[i], wo[i], preferred_element_type=jnp.float32)
        if i == 0:
            acc[...] = theirs
            ours_ref[...] = ours
        else:
            acc[...] += theirs
            ours_ref[...] += ours
    theirs_ref[...] = acc[...].astype(jnp.bfloat16)


def base_products(half, gathered, wa, wb, weight):
    count = HALF // DEPTH
    return pl.pallas_call(
        base_kernel,
        out_shape=[
            jax.ShapeDtypeStruct((ROWS, WIDTH), jnp.bfloat16),
            jax.ShapeDtypeStruct((ROWS, WIDTH), jnp.float32),
        ],
        in_specs=[SMEM, ANY, ANY, ANY, ANY],
        out_specs=[VMEM, VMEM],
        scratch_shapes=[
            pltpu.VMEM((count, ROWS, DEPTH), jnp.bfloat16),
            pltpu.VMEM((count, DEPTH, WIDTH), jnp.bfloat16),
            pltpu.VMEM((count, DEPTH, WIDTH), jnp.bfloat16),
            pltpu.VMEM((ROWS, WIDTH), jnp.float32),
            pltpu.SemaphoreType.DMA((count, 3)),
        ],
        compiler_params=vmem(53),
        cost_estimate=pl.CostEstimate(
            flops=4 * ROWS * HALF * WIDTH, bytes_accessed=10 << 20, transcendentals=0
        ),
    )(half, gathered, wa, wb, weight)


def add_kernel(ours_ref, recv_ref, out_ref):
    out_ref[...] = ours_ref[...] + recv_ref[...].astype(jnp.float32)


def add(ours, recv):
    return pl.pallas_call(
        add_kernel,
        out_shape=jax.ShapeDtypeStruct((ROWS, WIDTH), jnp.float32),
        in_specs=[VMEM, VMEM],
        out_specs=VMEM,
        compiler_params=vmem(8),
        cost_estimate=pl.CostEstimate(flops=1 << 17, bytes_accessed=2 << 20, transcendentals=0),
    )(ours, recv)


def last_kernel(low_ref, ups_ref, base_ref, out_ref):
    for k in range(4):
        row, col = (k % 2) * SEG, (k // 2) * RANK
        low = low_ref[row : row + SEG, col : col + RANK]
        up = jnp.dot(low, ups_ref[k], preferred_element_type=jnp.float32)
        rows = slice(k * SEG, (k + 1) * SEG)
        out_ref[rows, :] = (base_ref[rows, :] + 2.0 * up).astype(jnp.bfloat16)


def last_product(low, ups, base):
    return pl.pallas_call(
        last_kernel,
        out_shape=jax.ShapeDtypeStruct((ROWS, WIDTH), jnp.bfloat16),
        in_specs=[VMEM, VMEM, VMEM],
        out_specs=VMEM,
        compiler_params=vmem(8),
        cost_estimate=pl.CostEstimate(flops=1 << 24, bytes_accessed=2 << 20, transcendentals=0),
    )(low, ups, base)


def body(tokens, weight, down, up, segment_request, request_ids, stored_row):
    xl = lax.axis_index("xl").astype(jnp.int32)
    dp = lax.axis_index(DP).astype(jnp.int32)[None]
    place = jnp.stack([lax.axis_index("xh"), lax.axis_index("zl")]).astype(jnp.int32)

    spread = jnp.broadcast_to(request_ids[None, None, :], (PEERS, 1, 2))
    late_tokens, _ = lax.optimization_barrier((tokens, spread))
    gathered = lax.all_gather(late_tokens, ("y", "c"), axis=1, tiled=True)
    every_id = lax.all_to_all(spread, "zh", 0, 0, tiled=True)
    own, _ = lax.optimization_barrier((jnp.stack([down, up]), spread))
    pair = ("xh", "zl")
    far = [lax.ppermute(own, pair, [(i, i ^ flip) for i in range(4)]) for flip in (2, 1, 3)]

    sent = select(every_id, stored_row, place, own, *far)
    late_weight, _ = lax.optimization_barrier((weight, every_id))
    quarter = HALF // 2
    start = (1 - xl) * HALF
    wa = lax.ppermute(
        lax.dynamic_slice_in_dim(late_weight, start, quarter, 0), X, [(i, (i + 1) % 4) for i in range(4)]
    )
    wb = lax.ppermute(
        lax.dynamic_slice_in_dim(late_weight, start + quarter, quarter, 0),
        X,
        [(i, (i + 3) % 4) for i in range(4)],
    )

    got = lax.all_to_all(sent, "zh", 0, 0, tiled=True)

    partial = down_product(request_ids, stored_row, segment_request, dp, tokens, got)
    parts = lax.all_to_all(partial.reshape(32, 8, 128), TENSOR, 0, 0)
    low = lax.all_to_all(sum_parts(parts), TENSOR, 0, 0)

    weight, _ = lax.optimization_barrier((weight, partial))
    theirs, ours = base_products(xl[None], gathered, wa, wb, weight)
    recv = lax.ppermute(theirs, "xl", SWAP)
    ups = pick(request_ids, stored_row, segment_request, dp, got)
    return last_product(low.reshape(256, 128), ups, add(ours, recv))


def solution(mesh):
    fine = Mesh(mesh.devices.reshape(2, 4, 2, 2, 8, 2), ("xh", "zh", "zl", "xl", "y", "c"))
    in_specs = (
        P(DP, TENSOR),
        P(None, TENSOR),
        P(DP, None, TENSOR),
        P(DP, None, TENSOR),
        P(DP),
        P(DP),
        P(),
    )
    return jax.shard_map(body, mesh=fine, in_specs=in_specs, out_specs=P(DP, TENSOR), check_vma=False)
```

```python
import jax
import jax.numpy as jnp
from jax import lax
from jax.experimental import pallas as pl
from jax.experimental.pallas import tpu as pltpu
from jax.sharding import Mesh, PartitionSpec as P

SWAP = [(0, 1), (1, 0)]
DP = ("xh", "zh", "zl")
X = ("xh", "xl")
TENSOR = ("xl", "y", "c")
PEER_ORDER = ("c", "y", "xl")
ROWS = 512
SEG = 128
RANK = 64
WIDTH = 256
OWNED = 4
ZS = 8
PEERS = 4
HALF = 4096
DEPTH = 512

ANY = pl.BlockSpec(memory_space=pl.ANY)
SMEM = pl.BlockSpec(memory_space=pltpu.SMEM)
VMEM = pl.BlockSpec(memory_space=pltpu.VMEM)


def vmem(mib):
    return pltpu.CompilerParams(vmem_limit_bytes=mib << 20)


def select_kernel(ids_ref, stored_ref, place_ref, own_ref, x_ref, z_ref, xz_ref, out_ref, hold, sems):
    held = (own_ref, x_ref, z_ref, xz_ref)
    for zh in range(PEERS):
        for r in range(2):
            row = stored_ref[ids_ref[zh, 0, r]]
            slot = row % OWNED
            owner = row // OWNED
            across_x = owner // ZS != place_ref[0]
            across_z = owner % 2 != place_ref[1]
            which = across_x.astype(jnp.int32) + 2 * across_z.astype(jnp.int32)
            for j in range(4):

                @pl.when(which == j)
                def _(zh=zh, r=r, slot=slot, j=j):
                    for part in range(2):
                        hold[zh, 2 * r + part] = held[j][part, slot]
        pltpu.make_async_copy(hold.at[zh], out_ref.at[zh], sems.at[zh]).start()
    for zh in range(PEERS):
        pltpu.make_async_copy(hold.at[zh], out_ref.at[zh], sems.at[zh]).wait()


def select(ids, stored, place, own, x, z, xz):
    return pl.pallas_call(
        select_kernel,
        out_shape=jax.ShapeDtypeStruct((PEERS, 4, RANK, WIDTH), own.dtype),
        in_specs=[SMEM, SMEM, SMEM, VMEM, VMEM, VMEM, VMEM],
        out_specs=ANY,
        scratch_shapes=[
            pltpu.VMEM((PEERS, 4, RANK, WIDTH), own.dtype),
            pltpu.SemaphoreType.DMA((PEERS,)),
        ],
        compiler_params=vmem(8),
        cost_estimate=pl.CostEstimate(flops=0, bytes_accessed=2 << 20, transcendentals=0),
    )(ids, stored, place, own, x, z, xz)


def fetch(ids_ref, stored_ref, got_ref, mats, sems, part):
    copies = []
    for r in range(2):
        source = stored_ref[ids_ref[r]] // OWNED % ZS // 2
        copy = pltpu.make_async_copy(got_ref.at[source, 2 * r + part], mats.at[r], sems.at[r])
        copy.start()
        copies.append(copy)
    return copies


def down_kernel(ids_ref, stored_ref, seg_ref, dp_ref, tokens_ref, got_ref, out_ref, mats, sems):
    for copy in fetch(ids_ref, stored_ref, got_ref, mats, sems, 0):
        copy.wait()
    for k in range(4):
        part = lax.dot_general(
            tokens_ref[k * SEG : (k + 1) * SEG, :],
            mats[seg_ref[k] - 2 * dp_ref[0]],
            (((1,), (1,)), ((), ())),
            preferred_element_type=jnp.float32,
        )
        row, col = (k % 2) * SEG, (k // 2) * RANK
        out_ref[row : row + SEG, col : col + RANK] = part


def down_product(ids, stored, seg, dp, tokens, got):
    return pl.pallas_call(
        down_kernel,
        out_shape=jax.ShapeDtypeStruct((256, 128), jnp.float32),
        in_specs=[SMEM, SMEM, SMEM, SMEM, VMEM, ANY],
        out_specs=VMEM,
        scratch_shapes=[
            pltpu.VMEM((2, RANK, WIDTH), jnp.bfloat16),
            pltpu.SemaphoreType.DMA((2,)),
        ],
        compiler_params=vmem(4),
        cost_estimate=pl.CostEstimate(flops=1 << 24, bytes_accessed=1 << 20, transcendentals=0),
    )(ids, stored, seg, dp, tokens, got)


def pick_kernel(ids_ref, stored_ref, seg_ref, dp_ref, got_ref, out_ref, mats, sems):
    for copy in fetch(ids_ref, stored_ref, got_ref, mats, sems, 1):
        copy.wait()
    for k in range(4):
        out_ref[k] = mats[seg_ref[k] - 2 * dp_ref[0]]


def pick(ids, stored, seg, dp, got):
    return pl.pallas_call(
        pick_kernel,
        out_shape=jax.ShapeDtypeStruct((4, RANK, WIDTH), jnp.bfloat16),
        in_specs=[SMEM, SMEM, SMEM, SMEM, ANY],
        out_specs=VMEM,
        scratch_shapes=[
            pltpu.VMEM((2, RANK, WIDTH), jnp.bfloat16),
            pltpu.SemaphoreType.DMA((2,)),
        ],
        compiler_params=vmem(4),
        cost_estimate=pl.CostEstimate(flops=0, bytes_accessed=1 << 18, transcendentals=0),
    )(ids, stored, seg, dp, got)


def sum_kernel(parts_ref, out_ref):
    total = jnp.sum(parts_ref[...].astype(jnp.float32), axis=0).astype(jnp.bfloat16)
    out_ref[...] = jnp.broadcast_to(total[None], out_ref.shape)


def sum_parts(parts):
    return pl.pallas_call(
        sum_kernel,
        out_shape=jax.ShapeDtypeStruct(parts.shape, jnp.bfloat16),
        in_specs=[VMEM],
        out_specs=VMEM,
        compiler_params=vmem(4),
        cost_estimate=pl.CostEstimate(flops=0, bytes_accessed=128 << 20, transcendentals=0),
    )(parts)


def base_kernel(half_ref, t_ref, wa_ref, wb_ref, w_ref, theirs_ref, ours_ref, t, wt, wo, acc, sems):
    count = HALF // DEPTH
    per_quarter = count // 2
    copies = []
    for i in range(count):
        cols = slice(i * DEPTH, (i + 1) * DEPTH)
        source = wa_ref if i < per_quarter else wb_ref
        rows = pl.ds((i % per_quarter) * DEPTH, DEPTH)
        start = pl.multiple_of(half_ref[0] * HALF + i * DEPTH, DEPTH)
        trio = (
            pltpu.make_async_copy(t_ref.at[:, cols], t.at[i], sems.at[i, 0]),
            pltpu.make_async_copy(source.at[rows, :], wt.at[i], sems.at[i, 1]),
            pltpu.make_async_copy(w_ref.at[pl.ds(start, DEPTH), :], wo.at[i], sems.at[i, 2]),
        )
        for copy in trio:
            copy.start()
        copies.append(trio)
    for i in range(count):
        for copy in copies[i]:
            copy.wait()
        theirs = jnp.dot(t[i], wt[i], preferred_element_type=jnp.float32)
        ours = jnp.dot(t[i], wo[i], preferred_element_type=jnp.float32)
        if i == 0:
            acc[...] = theirs
            ours_ref[...] = ours
        else:
            acc[...] += theirs
            ours_ref[...] += ours
    theirs_ref[...] = acc[...].astype(jnp.bfloat16)


def base_products(half, gathered, wa, wb, weight):
    count = HALF // DEPTH
    return pl.pallas_call(
        base_kernel,
        out_shape=[
            jax.ShapeDtypeStruct((ROWS, WIDTH), jnp.bfloat16),
            jax.ShapeDtypeStruct((ROWS, WIDTH), jnp.float32),
        ],
        in_specs=[SMEM, ANY, ANY, ANY, ANY],
        out_specs=[VMEM, VMEM],
        scratch_shapes=[
            pltpu.VMEM((count, ROWS, DEPTH), jnp.bfloat16),
            pltpu.VMEM((count, DEPTH, WIDTH), jnp.bfloat16),
            pltpu.VMEM((count, DEPTH, WIDTH), jnp.bfloat16),
            pltpu.VMEM((ROWS, WIDTH), jnp.float32),
            pltpu.SemaphoreType.DMA((count, 3)),
        ],
        compiler_params=vmem(53),
        cost_estimate=pl.CostEstimate(
            flops=4 * ROWS * HALF * WIDTH, bytes_accessed=10 << 20, transcendentals=0
        ),
    )(half, gathered, wa, wb, weight)


def add_kernel(ours_ref, recv_ref, out_ref):
    out_ref[...] = ours_ref[...] + recv_ref[...].astype(jnp.float32)


def add(ours, recv):
    return pl.pallas_call(
        add_kernel,
        out_shape=jax.ShapeDtypeStruct((ROWS, WIDTH), jnp.float32),
        in_specs=[VMEM, VMEM],
        out_specs=VMEM,
        compiler_params=vmem(8),
        cost_estimate=pl.CostEstimate(flops=1 << 17, bytes_accessed=2 << 20, transcendentals=0),
    )(ours, recv)


def last_kernel(low_ref, ups_ref, base_ref, out_ref):
    for k in range(4):
        row, col = (k % 2) * SEG, (k // 2) * RANK
        low = low_ref[row : row + SEG, col : col + RANK]
        up = jnp.dot(low, ups_ref[k], preferred_element_type=jnp.float32)
        rows = slice(k * SEG, (k + 1) * SEG)
        out_ref[rows, :] = (base_ref[rows, :] + 2.0 * up).astype(jnp.bfloat16)


def last_product(low, ups, base):
    return pl.pallas_call(
        last_kernel,
        out_shape=jax.ShapeDtypeStruct((ROWS, WIDTH), jnp.bfloat16),
        in_specs=[VMEM, VMEM, VMEM],
        out_specs=VMEM,
        compiler_params=vmem(8),
        cost_estimate=pl.CostEstimate(flops=1 << 24, bytes_accessed=2 << 20, transcendentals=0),
    )(low, ups, base)


def body(tokens, weight, down, up, segment_request, request_ids, stored_row):
    xl = lax.axis_index("xl").astype(jnp.int32)
    dp = lax.axis_index(DP).astype(jnp.int32)[None]
    place = jnp.stack([lax.axis_index("xh"), lax.axis_index("zl")]).astype(jnp.int32)

    spread = jnp.broadcast_to(request_ids[None, None, :], (PEERS, 1, 2))
    late_tokens, _ = lax.optimization_barrier((tokens, spread))
    gathered = lax.all_gather(late_tokens, ("y", "c"), axis=1, tiled=True)
    every_id = lax.all_to_all(spread, "zh", 0, 0, tiled=True)
    own, _ = lax.optimization_barrier((jnp.stack([down, up]), spread))
    pair = ("xh", "zl")
    far = [lax.ppermute(own, pair, [(i, i ^ flip) for i in range(4)]) for flip in (2, 1, 3)]

    sent = select(every_id, stored_row, place, own, *far)
    late_weight, _ = lax.optimization_barrier((weight, every_id))
    quarter = HALF // 2
    start = (1 - xl) * HALF
    wa = lax.ppermute(
        lax.dynamic_slice_in_dim(late_weight, start, quarter, 0), X, [(i, (i + 1) % 4) for i in range(4)]
    )
    wb = lax.ppermute(
        lax.dynamic_slice_in_dim(late_weight, start + quarter, quarter, 0),
        X,
        [(i, (i + 3) % 4) for i in range(4)],
    )

    got = lax.all_to_all(sent, "zh", 0, 0, tiled=True)

    partial = down_product(request_ids, stored_row, segment_request, dp, tokens, got)
    parts = lax.all_to_all(partial.reshape(32, 8, 128), PEER_ORDER, 0, 0)
    low = lax.all_to_all(sum_parts(parts), PEER_ORDER, 0, 0)

    weight, _ = lax.optimization_barrier((weight, partial))
    theirs, ours = base_products(xl[None], gathered, wa, wb, weight)
    recv = lax.ppermute(theirs, "xl", SWAP)
    ups = pick(request_ids, stored_row, segment_request, dp, got)
    return last_product(low.reshape(256, 128), ups, add(ours, recv))


def solution(mesh):
    fine = Mesh(mesh.devices.reshape(2, 4, 2, 2, 8, 2), ("xh", "zh", "zl", "xl", "y", "c"))
    in_specs = (
        P(DP, TENSOR),
        P(None, TENSOR),
        P(DP, None, TENSOR),
        P(DP, None, TENSOR),
        P(DP),
        P(DP),
        P(),
    )
    return jax.shard_map(body, mesh=fine, in_specs=in_specs, out_specs=P(DP, TENSOR), check_vma=False)
```

```python
import jax
import jax.numpy as jnp
from jax import lax
from jax.experimental import pallas as pl
from jax.experimental.pallas import tpu as pltpu
from jax.sharding import Mesh, PartitionSpec as P

SWAP = [(0, 1), (1, 0)]
DP = ("xh", "zh", "zl")
X = ("xh", "xl")
TENSOR = ("xl", "y", "c")
PEER_ORDER = ("c", "y", "xl")
ROWS = 512
SEG = 128
RANK = 64
WIDTH = 256
OWNED = 4
ZS = 8
PEERS = 4
HALF = 4096
DEPTH = 512

ANY = pl.BlockSpec(memory_space=pl.ANY)
SMEM = pl.BlockSpec(memory_space=pltpu.SMEM)
VMEM = pl.BlockSpec(memory_space=pltpu.VMEM)


def vmem(mib):
    return pltpu.CompilerParams(vmem_limit_bytes=mib << 20)


def select_kernel(ids_ref, stored_ref, place_ref, own_ref, x_ref, z_ref, xz_ref, out_ref, hold, sems):
    held = (own_ref, x_ref, z_ref, xz_ref)
    for zh in range(PEERS):
        for r in range(2):
            row = stored_ref[ids_ref[zh, 0, r]]
            slot = row % OWNED
            owner = row // OWNED
            across_x = owner // ZS != place_ref[0]
            across_z = owner % 2 != place_ref[1]
            which = across_x.astype(jnp.int32) + 2 * across_z.astype(jnp.int32)
            for j in range(4):

                @pl.when(which == j)
                def _(zh=zh, r=r, slot=slot, j=j):
                    for part in range(2):
                        hold[zh, 2 * r + part] = held[j][part, slot]
        pltpu.make_async_copy(hold.at[zh], out_ref.at[zh], sems.at[zh]).start()
    for zh in range(PEERS):
        pltpu.make_async_copy(hold.at[zh], out_ref.at[zh], sems.at[zh]).wait()


def select(ids, stored, place, own, x, z, xz):
    return pl.pallas_call(
        select_kernel,
        out_shape=jax.ShapeDtypeStruct((PEERS, 4, RANK, WIDTH), own.dtype),
        in_specs=[SMEM, SMEM, SMEM, VMEM, VMEM, VMEM, VMEM],
        out_specs=ANY,
        scratch_shapes=[
            pltpu.VMEM((PEERS, 4, RANK, WIDTH), own.dtype),
            pltpu.SemaphoreType.DMA((PEERS,)),
        ],
        compiler_params=vmem(8),
        cost_estimate=pl.CostEstimate(flops=0, bytes_accessed=2 << 20, transcendentals=0),
    )(ids, stored, place, own, x, z, xz)


def fetch(ids_ref, stored_ref, got_ref, mats, sems, part):
    copies = []
    for r in range(2):
        source = stored_ref[ids_ref[r]] // OWNED % ZS // 2
        copy = pltpu.make_async_copy(got_ref.at[source, 2 * r + part], mats.at[r], sems.at[r])
        copy.start()
        copies.append(copy)
    return copies


def down_kernel(ids_ref, stored_ref, seg_ref, dp_ref, tokens_ref, got_ref, out_ref, mats, sems):
    for copy in fetch(ids_ref, stored_ref, got_ref, mats, sems, 0):
        copy.wait()
    for k in range(4):
        part = lax.dot_general(
            tokens_ref[k * SEG : (k + 1) * SEG, :],
            mats[seg_ref[k] - 2 * dp_ref[0]],
            (((1,), (1,)), ((), ())),
            preferred_element_type=jnp.float32,
        )
        row, col = (k % 2) * SEG, (k // 2) * RANK
        out_ref[row : row + SEG, col : col + RANK] = part


def down_product(ids, stored, seg, dp, tokens, got):
    return pl.pallas_call(
        down_kernel,
        out_shape=jax.ShapeDtypeStruct((256, 128), jnp.float32),
        in_specs=[SMEM, SMEM, SMEM, SMEM, VMEM, ANY],
        out_specs=VMEM,
        scratch_shapes=[
            pltpu.VMEM((2, RANK, WIDTH), jnp.bfloat16),
            pltpu.SemaphoreType.DMA((2,)),
        ],
        compiler_params=vmem(4),
        cost_estimate=pl.CostEstimate(flops=1 << 24, bytes_accessed=1 << 20, transcendentals=0),
    )(ids, stored, seg, dp, tokens, got)


def pick_kernel(ids_ref, stored_ref, seg_ref, dp_ref, got_ref, out_ref, mats, sems):
    for copy in fetch(ids_ref, stored_ref, got_ref, mats, sems, 1):
        copy.wait()
    for k in range(4):
        out_ref[k] = mats[seg_ref[k] - 2 * dp_ref[0]]


def pick(ids, stored, seg, dp, got):
    return pl.pallas_call(
        pick_kernel,
        out_shape=jax.ShapeDtypeStruct((4, RANK, WIDTH), jnp.bfloat16),
        in_specs=[SMEM, SMEM, SMEM, SMEM, ANY],
        out_specs=VMEM,
        scratch_shapes=[
            pltpu.VMEM((2, RANK, WIDTH), jnp.bfloat16),
            pltpu.SemaphoreType.DMA((2,)),
        ],
        compiler_params=vmem(4),
        cost_estimate=pl.CostEstimate(flops=0, bytes_accessed=1 << 18, transcendentals=0),
    )(ids, stored, seg, dp, got)


def sum_kernel(parts_ref, out_ref):
    total = jnp.sum(parts_ref[...].astype(jnp.float32), axis=0).astype(jnp.bfloat16)
    out_ref[...] = jnp.broadcast_to(total[None], out_ref.shape)


def sum_parts(parts):
    return pl.pallas_call(
        sum_kernel,
        out_shape=jax.ShapeDtypeStruct(parts.shape, jnp.bfloat16),
        in_specs=[VMEM],
        out_specs=VMEM,
        compiler_params=vmem(4),
        cost_estimate=pl.CostEstimate(flops=0, bytes_accessed=128 << 20, transcendentals=0),
    )(parts)


def base_kernel(half_ref, t_ref, wa_ref, wb_ref, w_ref, theirs_ref, ours_ref, t, wt, wo, acc, sems):
    count = HALF // DEPTH
    per_quarter = count // 2
    copies = []
    for i in range(count):
        cols = slice(i * DEPTH, (i + 1) * DEPTH)
        source = wa_ref if i < per_quarter else wb_ref
        rows = pl.ds((i % per_quarter) * DEPTH, DEPTH)
        start = pl.multiple_of(half_ref[0] * HALF + i * DEPTH, DEPTH)
        trio = (
            pltpu.make_async_copy(t_ref.at[:, cols], t.at[i], sems.at[i, 0]),
            pltpu.make_async_copy(source.at[rows, :], wt.at[i], sems.at[i, 1]),
            pltpu.make_async_copy(w_ref.at[pl.ds(start, DEPTH), :], wo.at[i], sems.at[i, 2]),
        )
        for copy in trio:
            copy.start()
        copies.append(trio)
    for i in range(count):
        for copy in copies[i]:
            copy.wait()
        theirs = jnp.dot(t[i], wt[i], preferred_element_type=jnp.float32)
        ours = jnp.dot(t[i], wo[i], preferred_element_type=jnp.float32)
        if i == 0:
            acc[...] = theirs
            ours_ref[...] = ours
        else:
            acc[...] += theirs
            ours_ref[...] += ours
    theirs_ref[...] = acc[...].astype(jnp.bfloat16)


def base_products(half, gathered, wa, wb, weight):
    count = HALF // DEPTH
    return pl.pallas_call(
        base_kernel,
        out_shape=[
            jax.ShapeDtypeStruct((ROWS, WIDTH), jnp.bfloat16),
            jax.ShapeDtypeStruct((ROWS, WIDTH), jnp.float32),
        ],
        in_specs=[SMEM, ANY, ANY, ANY, ANY],
        out_specs=[VMEM, VMEM],
        scratch_shapes=[
            pltpu.VMEM((count, ROWS, DEPTH), jnp.bfloat16),
            pltpu.VMEM((count, DEPTH, WIDTH), jnp.bfloat16),
            pltpu.VMEM((count, DEPTH, WIDTH), jnp.bfloat16),
            pltpu.VMEM((ROWS, WIDTH), jnp.float32),
            pltpu.SemaphoreType.DMA((count, 3)),
        ],
        compiler_params=vmem(54),
        cost_estimate=pl.CostEstimate(
            flops=4 * ROWS * HALF * WIDTH, bytes_accessed=10 << 20, transcendentals=0
        ),
    )(half, gathered, wa, wb, weight)


def add_kernel(ours_ref, recv_ref, out_ref):
    out_ref[...] = ours_ref[...] + recv_ref[...].astype(jnp.float32)


def add(ours, recv):
    return pl.pallas_call(
        add_kernel,
        out_shape=jax.ShapeDtypeStruct((ROWS, WIDTH), jnp.float32),
        in_specs=[VMEM, VMEM],
        out_specs=VMEM,
        compiler_params=vmem(8),
        cost_estimate=pl.CostEstimate(flops=1 << 17, bytes_accessed=2 << 20, transcendentals=0),
    )(ours, recv)


def last_kernel(low_ref, ups_ref, base_ref, out_ref):
    for k in range(4):
        row, col = (k % 2) * SEG, (k // 2) * RANK
        low = low_ref[row : row + SEG, col : col + RANK]
        up = jnp.dot(low, ups_ref[k], preferred_element_type=jnp.float32)
        rows = slice(k * SEG, (k + 1) * SEG)
        out_ref[rows, :] = (base_ref[rows, :] + 2.0 * up).astype(jnp.bfloat16)


def last_product(low, ups, base):
    return pl.pallas_call(
        last_kernel,
        out_shape=jax.ShapeDtypeStruct((ROWS, WIDTH), jnp.bfloat16),
        in_specs=[VMEM, VMEM, VMEM],
        out_specs=VMEM,
        compiler_params=vmem(8),
        cost_estimate=pl.CostEstimate(flops=1 << 24, bytes_accessed=2 << 20, transcendentals=0),
    )(low, ups, base)


def body(tokens, weight, down, up, segment_request, request_ids, stored_row):
    xl = lax.axis_index("xl").astype(jnp.int32)
    dp = lax.axis_index(DP).astype(jnp.int32)[None]
    place = jnp.stack([lax.axis_index("xh"), lax.axis_index("zl")]).astype(jnp.int32)

    spread = jnp.broadcast_to(request_ids[None, None, :], (PEERS, 1, 2))
    late_tokens, _ = lax.optimization_barrier((tokens, spread))
    gathered = lax.all_gather(late_tokens, ("y", "c"), axis=1, tiled=True)
    every_id = lax.all_to_all(spread, "zh", 0, 0, tiled=True)
    own, _ = lax.optimization_barrier((jnp.stack([down, up]), spread))
    pair = ("xh", "zl")
    far = [lax.ppermute(own, pair, [(i, i ^ flip) for i in range(4)]) for flip in (2, 1, 3)]

    sent = select(every_id, stored_row, place, own, *far)
    late_weight, _ = lax.optimization_barrier((weight, every_id))
    quarter = HALF // 2
    start = (1 - xl) * HALF
    wa = lax.ppermute(
        lax.dynamic_slice_in_dim(late_weight, start, quarter, 0), X, [(i, (i + 1) % 4) for i in range(4)]
    )
    wb = lax.ppermute(
        lax.dynamic_slice_in_dim(late_weight, start + quarter, quarter, 0),
        X,
        [(i, (i + 3) % 4) for i in range(4)],
    )

    got = lax.all_to_all(sent, "zh", 0, 0, tiled=True)

    partial = down_product(request_ids, stored_row, segment_request, dp, tokens, got)
    parts = lax.all_to_all(partial.reshape(32, 8, 128), PEER_ORDER, 0, 0)
    low = lax.all_to_all(sum_parts(parts), PEER_ORDER, 0, 0)

    weight, _ = lax.optimization_barrier((weight, partial))
    theirs, ours = base_products(xl[None], gathered, wa, wb, weight)
    recv = lax.ppermute(theirs, "xl", SWAP)
    ups = pick(request_ids, stored_row, segment_request, dp, got)
    return last_product(low.reshape(256, 128), ups, add(ours, recv))


def solution(mesh):
    fine = Mesh(mesh.devices.reshape(2, 4, 2, 2, 8, 2), ("xh", "zh", "zl", "xl", "y", "c"))
    in_specs = (
        P(DP, TENSOR),
        P(None, TENSOR),
        P(DP, None, TENSOR),
        P(DP, None, TENSOR),
        P(DP),
        P(DP),
        P(),
    )
    return jax.shard_map(body, mesh=fine, in_specs=in_specs, out_specs=P(DP, TENSOR), check_vma=False)
```
